128 devices in a mesh: row: 8 (over z, core), col: 16 (over x, y).
Axes of the slice: x: 4, y: 4, z: 4, core: 2. Of those that a mesh axis runs over, the one named last changes fastest.
Arguments:
- features: bfloat16 [256, 512, 256], P('row', 'col'), may hold values from -6 to 6
- conv_weight: bfloat16 [3, 3, 256, 256], replicated, may hold values from -0.125 to 0.125
- first_weight: bfloat16 [12544, 1024], P(('row', 'col')), may hold values from -0.0546875 to 0.0546875
- second_weight: bfloat16 [1024, 1024], replicated, may hold values from -0.1875 to 0.1875
- out_weight: bfloat16 [1024, 42], replicated, may hold values from -0.1875 to 0.1875
- roi_count: int32 [128], P(('row', 'col')), may hold values from 32 to 256, as said below
- roi_row: int32 [32768], P(('row', 'col')), may hold values from 4 to 27
- roi_col: int32 [32768], P(('row', 'col')), may hold values from 4 to 27
- roi_angle: int32 [32768], P(('row', 'col')), may hold values from 0 to 7
- roi_label: int32 [32768], P(('row', 'col')), may hold values from 0 to 37
- roi_target: bfloat16 [32768, 5], P(('row', 'col')), may hold values from -4 to 4
Outputs:
- neck: bfloat16 [256, 512, 256], P('row', 'col')
- feat_grad: float32 [256, 512, 256], P('row', 'col')
- second_grad: float32 [1024, 1024], replicated
- out_grad: float32 [1024, 42], replicated
The draws below stay inside these ranges and needn't reach their ends.
Inputs may be any that keep to these rules, and one draw needn't show every extreme that they name: `roi_count`: A tile's live RoIs fill its first slots; in every draw some tile has all 256 slots live.
All inputs are finite; a program needn't handle non-finite values.
Results may differ from the reference program's by a relative error of at most 0.01.
Values may be sent and summed in bfloat16 or wider, within the bound.
A program may use at most 192 MiB of HBM per device.

```python
import math
import jax
import jax.numpy as jnp
import numpy as np
from jax import lax

C = 256
POOL = 7
ANGLES = 8
HID = 1024
CLS = 37
BOXP = 5
TH = 32
TW = 32
R_DEV = 256
F = 12544
OUTW = 42
TILES = 128
NH = 256
NW = 512
ROIS = 32768
N_ROW = 8
N_COL = 16


def draw_roi_count(key, part):
    key = jax.random.fold_in(key, 11)
    key_base, key_crowd, key_forced = jax.random.split(key, 3)
    base = jax.random.randint(key_base, (TILES,), R_DEV // 8, R_DEV // 2 + 1)
    crowded = jax.random.randint(key_crowd, (TILES,), 0, 4) == 0
    forced = jax.random.randint(key_forced, (), 0, TILES)
    crowded = crowded | (jnp.arange(TILES) == forced)
    return jnp.where(crowded, R_DEV, base).astype(jnp.int32)


def draw_roi_label(key, part):
    key = jax.random.fold_in(key, 13)
    key_shift, key_pick, key_other = jax.random.split(key, 3)
    shift = jax.random.randint(key_shift, (), 0, CLS)
    home = (jnp.arange(TILES, dtype=jnp.int32) + shift) % CLS
    home_rows = jnp.repeat(home, R_DEV)
    pick = jax.random.randint(key_pick, (ROIS,), 0, 8) < 7
    other = jax.random.randint(key_other, (ROIS,), 0, CLS + 1)
    return jnp.where(pick, home_rows, other).astype(jnp.int32)


def with_ends(entries, rng, smallest, top_value):
    longest = entries.shape.index(max(entries.shape))
    spots = []
    for shift in (0, 1):
        where = [jax.random.randint(jax.random.fold_in(rng, axis), (), 0, length) for axis, length in enumerate(entries.shape)]
        where[longest] = (where[longest] + shift) % entries.shape[longest]
        spots.append(tuple(where))
    return entries.at[spots[0]].set(smallest).at[spots[1]].set(top_value)


def steps_of(key, dims, pieces, least, top_value):
    level, own = 1.0, jax.random.fold_in(key, 6)
    for position, parts in pieces:
        draws = jnp.exp(jax.random.uniform(jax.random.fold_in(own, position), (parts,), jnp.float32, least / len(pieces), top_value / len(pieces)))
        level = level * jnp.repeat(draws, dims[position] // parts).reshape([-1 if axis == position else 1 for axis in range(len(dims))])
    return level


def normal_values(key, dims, deviation, bound, pieces=(), held_as=jnp.bfloat16):
    result = deviation * jax.random.normal(key, dims, jnp.float32)
    if pieces:
        result = result * steps_of(key, dims, pieces, -0.22, 0.18)
    return jnp.clip(result, -bound, bound).astype(held_as)


def setup_inputs(seed: int = 0) -> dict:
    seeds = jax.random.split(jax.random.key(seed), 12)
    features = normal_values(seeds[0], (NH, NW, C), 1.0, 6.0, ((0, 8), (1, 16)))
    conv_weight = normal_values(seeds[1], (3, 3, C, C), (9 * C) ** -0.5, 0.125)
    first_weight = normal_values(seeds[2], (F, HID), F ** -0.5, 0.0546875, ((0, 128),))
    second_weight = normal_values(seeds[3], (HID, HID), HID ** -0.5, 0.1875)
    out_weight = normal_values(seeds[4], (HID, OUTW), HID ** -0.5, 0.1875)
    roi_count = draw_roi_count(jax.random.fold_in(seeds[11], 71), 0)
    roi_row = with_ends(jax.random.randint(seeds[6], (ROIS,), 4, TH - 4), jax.random.fold_in(seeds[6], 1), 4, (TH - 4) - 1).astype(jnp.int32)
    roi_col = with_ends(jax.random.randint(seeds[7], (ROIS,), 4, TW - 4), jax.random.fold_in(seeds[7], 1), 4, (TW - 4) - 1).astype(jnp.int32)
    roi_angle = with_ends(jax.random.randint(seeds[8], (ROIS,), 0, ANGLES), jax.random.fold_in(seeds[8], 1), 0, ANGLES - 1).astype(jnp.int32)
    roi_label = draw_roi_label(jax.random.fold_in(seeds[11], 71), 0)
    roi_target = normal_values(seeds[10], (ROIS, BOXP), 1.0, 4.0, ((0, 128),))
    return {"features": features, "conv_weight": conv_weight, "first_weight": first_weight, "second_weight": second_weight, "out_weight": out_weight, "roi_count": roi_count, "roi_row": roi_row, "roi_col": roi_col, "roi_angle": roi_angle, "roi_label": roi_label, "roi_target": roi_target}


prior_logit = -4.59512

def offset_tables(pool, angles):
    turn = np.arange(angles) * math.pi / angles
    along = np.arange(pool) - pool // 2
    down = (along[:, None] * np.ones((1, pool))).reshape(1, -1)
    across = (np.ones((pool, 1)) * along[None, :]).reshape(1, -1)
    cosine = np.cos(turn)[:, None]
    sine = np.sin(turn)[:, None]
    shift_rows = np.floor(down * cosine - across * sine + 0.5).astype(np.int32)
    shift_cols = np.floor(down * sine + across * cosine + 0.5).astype(np.int32)
    return (shift_rows, shift_cols)

def sample_cells(centre_row, centre_col, angle, width):
    shift_rows, shift_cols = offset_tables(POOL, ANGLES)
    choose = (angle[:, None] == jnp.arange(ANGLES, dtype=jnp.int32)[None, :]).astype(jnp.int32)
    drow = lax.optimization_barrier(jnp.sum(choose[:, :, None] * jnp.asarray(shift_rows)[None], axis=1))
    dcol = lax.optimization_barrier(jnp.sum(choose[:, :, None] * jnp.asarray(shift_cols)[None], axis=1))
    return ((centre_row[:, None] + drow) * width + centre_col[:, None] + dcol).astype(jnp.int32)

def slope(value):
    return 0.5 * (1.0 + jax.scipy.special.erf(value / math.sqrt(2.0))) + value * jnp.exp(-0.5 * value * value) / math.sqrt(2.0 * math.pi)

def head_block(blocks, labels, targets, live, first_w, second_w, out_w):
    classes = out_w.shape[1] - targets.shape[1]
    pre1 = jnp.dot(blocks, first_w, preferred_element_type=jnp.float32)
    hid1 = jax.nn.gelu(pre1, approximate=False).astype(jnp.bfloat16)
    pre2 = jnp.dot(hid1, second_w, preferred_element_type=jnp.float32)
    hid2 = jax.nn.gelu(pre2, approximate=False).astype(jnp.bfloat16)
    z = jnp.dot(hid2, out_w, preferred_element_type=jnp.float32)
    onehot = (labels[:, None] == jnp.arange(classes, dtype=jnp.int32)[None, :]).astype(jnp.float32)
    foreground = (labels < classes).astype(jnp.float32)[:, None]
    dlogit = jax.nn.sigmoid(z[:, :classes] + prior_logit) - onehot
    dbox = jnp.clip(z[:, classes:] - targets.astype(jnp.float32), -1.0, 1.0) * foreground
    dz = jnp.where(live[:, None], jnp.concatenate([dlogit, dbox], axis=1), 0.0).astype(jnp.bfloat16)
    contract_rows = (((0,), (0,)), ((), ()))
    contract_cols = (((1,), (1,)), ((), ()))
    out_grad = lax.dot_general(hid2, dz, contract_rows, preferred_element_type=jnp.float32)
    dpre2 = (lax.dot_general(dz, out_w, contract_cols, preferred_element_type=jnp.float32) * slope(pre2)).astype(jnp.bfloat16)
    second_grad = lax.dot_general(hid1, dpre2, contract_rows, preferred_element_type=jnp.float32)
    dpre1 = (lax.dot_general(dpre2, second_w, contract_cols, preferred_element_type=jnp.float32) * slope(pre1)).astype(jnp.bfloat16)
    dblocks = lax.dot_general(dpre1, first_w, contract_cols, preferred_element_type=jnp.float32).astype(jnp.bfloat16)
    return (dblocks, second_grad, out_grad)

def reference(features, conv_weight, first_weight, second_weight, out_weight, roi_count, roi_row, roi_col, roi_angle, roi_label, roi_target):
    padded = jnp.pad(features, ((1, 1), (1, 1), (0, 0)))
    total = jnp.zeros((NH * NW, C), jnp.float32)
    for first in range(3):
        for second in range(3):
            window = padded[first:first + NH, second:second + NW, :].reshape(NH * NW, C)
            total = total + jnp.dot(window, conv_weight[first, second], preferred_element_type=jnp.float32)
    neck = total.astype(jnp.bfloat16).reshape(NH, NW, C)

    def per_tile(carry, tile):
        tile_row = tile // N_COL
        tile_col = tile % N_COL
        block = lax.dynamic_slice(neck, (tile_row * TH, tile_col * TW, jnp.zeros((), jnp.int32)), (TH, TW, C)).reshape(TH * TW, C)
        start = (tile * R_DEV).astype(jnp.int32)
        cells = sample_cells(lax.dynamic_slice_in_dim(roi_row, start, R_DEV, 0), lax.dynamic_slice_in_dim(roi_col, start, R_DEV, 0), lax.dynamic_slice_in_dim(roi_angle, start, R_DEV, 0), TW)
        blocks = jnp.take(block, cells.reshape(-1), axis=0).reshape(R_DEV, F)
        labels = lax.dynamic_slice_in_dim(roi_label, start, R_DEV, 0)
        targets = lax.dynamic_slice_in_dim(roi_target, start, R_DEV, 0)
        live = jnp.arange(R_DEV, dtype=jnp.int32) < roi_count[tile]
        dblocks, second_part, out_part = head_block(blocks, labels, targets, live, first_weight, second_weight, out_weight)
        grad_tile = jnp.zeros((TH * TW, C), jnp.float32).at[cells.reshape(-1)].add(dblocks.reshape(R_DEV * POOL * POOL, C).astype(jnp.float32))
        return ((carry[0] + second_part, carry[1] + out_part), grad_tile)
    init = (jnp.zeros((HID, HID), jnp.float32), jnp.zeros((HID, OUTW), jnp.float32))
    (second_grad, out_grad), grads = lax.scan(per_tile, init, jnp.arange(TILES, dtype=jnp.int32))
    feat_grad = grads.reshape(N_ROW, N_COL, TH, TW, C).transpose(0, 2, 1, 3, 4).reshape(NH, NW, C)
    return (neck, feat_grad, second_grad, out_grad)
```

```python
import functools
import math

import jax
import jax.numpy as jnp
import numpy as np
from jax import lax
from jax.experimental import pallas as pl
from jax.experimental.pallas import tpu as pltpu
from jax.sharding import PartitionSpec as P

POOL = 7
ANGLES = 8
CLASSES = 37
OUTS = 42
HID = 1024
CH = 256
CELLS = 1024
ROIS = 256
SAMPLES = POOL * POOL
GROUP = 784
SPAN = POOL * CH
WIDE = HID + 128
COLS = WIDE // 3
MESH = pl.DeviceIdType.MESH

prior_logit = -4.59512

PARTS = (
    (0, 128, 256, "xyz"),
    (256, 128, 256, "yzx"),
    (512, 144, 272, "zxy"),
)


def offset_tables(pool, angles):
    turn = np.arange(angles) * math.pi / angles
    along = np.arange(pool) - pool // 2
    down = (along[:, None] * np.ones((1, pool))).reshape(1, -1)
    across = (np.ones((pool, 1)) * along[None, :]).reshape(1, -1)
    cosine = np.cos(turn)[:, None]
    sine = np.sin(turn)[:, None]
    shift_rows = np.floor(down * cosine - across * sine + 0.5).astype(np.int32)
    shift_cols = np.floor(down * sine + across * cosine + 0.5).astype(np.int32)
    return (shift_rows, shift_cols)


def erf_parts(value):
    return 0.5 * (1.0 + lax.erf(value * math.sqrt(0.5)))


def slope(value, phi):
    return phi + value * jnp.exp(-0.5 * value * value) * (1.0 / math.sqrt(2.0 * math.pi))


def dot(a, b):
    return jnp.dot(a, b, preferred_element_type=jnp.float32)


def dot_nt(a, b):
    return lax.dot_general(a, b, (((1,), (1,)), ((), ())), preferred_element_type=jnp.float32)


def dot_tn(a, b):
    return lax.dot_general(a, b, (((0,), (0,)), ((), ())), preferred_element_type=jnp.float32)


def kernel(
    feat,
    edge_cols,
    conv_w,
    shard,
    w2,
    wo,
    meta,
    meta_t,
    table,
    table_t,
    neck,
    feat_grad,
    total,
    wf,
    stage,
    slots,
    halo_row,
    halo_col,
    halo_corner,
    side,
    ext,
    taps,
    x,
    cells_t,
    pre1,
    gp1,
    pre2,
    gp2,
    hid1,
    dpre2,
    dpre1,
    dxs,
    keep,
    send0,
    recv0,
    send1,
    recv1,
    keep1,
    send2,
    recv2,
    keep2,
    recv3,
    halo_s,
    halo_r,
    group_s,
    group_r,
    ring_s,
    ring_r,
    sib_s,
    sib_r,
    red_s,
    red_r,
):
    row = lax.axis_index("row")
    col = lax.axis_index("col")
    pos = {"x": col // 4, "y": lax.rem(col, 4), "z": row // 2}
    core = lax.rem(row, 2)

    def device(axis, step):
        at = dict(pos)
        at[axis] = lax.rem(pos[axis] + (step + 4), 4)
        return (at["z"] * 2 + core, at["x"] * 4 + at["y"])

    sibling = (row + 1 - 2 * core, col)
    member = lax.rem(col, 8)

    def group_device(step):
        return (row, col - member + lax.rem(member + step, 8))

    around = [(a, b) for a in (-1, 0, 1) for b in (-1, 0, 1) if (a, b) != (0, 0)]

    def halo_device(a, b):
        return (lax.rem(row + a + 8, 8), lax.rem(col + b + 16, 16))

    barrier = pltpu.get_barrier_semaphore()
    partners = [sibling] + [device(axis, step) for axis in "xyz" for step in (1, 2, 3)]
    partners += [group_device(step) for step in range(1, 8)]
    partners += [halo_device(a, b) for a, b in around]
    for partner in partners:
        pl.semaphore_signal(barrier, inc=1, device_id=partner, device_id_type=MESH)
    pl.semaphore_wait(barrier, len(partners))

    def remote(src, dst, send_sem, recv_sem, target):
        return pltpu.make_async_remote_copy(
            src_ref=src,
            dst_ref=dst,
            send_sem=send_sem,
            recv_sem=recv_sem,
            device_id=target,
            device_id_type=MESH,
        )

    def group_copy(step):
        other = lax.rem(member + step, 8)
        return remote(
            stage.at[other], slots.at[member], group_s.at[step - 1], group_r.at[step - 1], group_device(step)
        )

    for m in range(8):
        stage[m, 0:98, :] = shard[:, 128 * m : 128 * m + 128]
    group_copies = [group_copy(step) for step in range(1, 8)]
    for copy in group_copies:
        copy.start()

    def halo_copy(index):
        a, b = around[index]
        if b == 0:
            src, dst = feat.at[0 if a < 0 else 31], halo_row.at[0 if a > 0 else 1]
        elif a == 0:
            src, dst = edge_cols.at[0 if b < 0 else 1], halo_col.at[0 if b > 0 else 1]
        else:
            src = feat.at[0 if a < 0 else 31, pl.ds(0 if b < 0 else 16, 16)]
            dst = halo_corner.at[0 if a > 0 else 1, 0 if b > 0 else 1]
        return remote(src, dst, halo_s.at[index], halo_r.at[index], halo_device(a, b))

    halo_copies = [halo_copy(index) for index in range(8)]
    for copy in halo_copies:
        copy.start()

    def region(at, first, count):
        def one(axis):
            return slice(None) if at[axis] is None else at[axis]

        if at["x"] is None:
            low, high = slice(None), slice(None)
        else:
            low, high = lax.rem(at["x"], 2), at["x"] // 2
        return wf.at[low, one("y"), one("z"), core, high, pl.ds(first, count)]

    def held(part, phase, step):
        order = PARTS[part][3]
        at = dict(pos)
        for axis in order[:phase]:
            at[axis] = None
        at[order[phase]] = lax.rem(pos[order[phase]] + (step + 4), 4)
        return at

    def ring_copies(part, phase, half):
        first, cut, count, order = PARTS[part]
        axis = order[phase]
        copies = []
        for way, step in ((0, 1), (1, -1)):
            sem = ((part * 3 + phase) * 2 + half) * 2 + way
            if half == 0:
                ref = region(held(part, phase, 0), first, count)
            elif way == 0:
                ref = region(held(part, phase, -1), first, cut)
            else:
                ref = region(held(part, phase, 1), first + cut, count - cut)
            copies.append(remote(ref, ref, ring_s.at[sem], ring_r.at[sem], device(axis, step)))
        return copies

    def sib_copy(part, phase, step):
        first, cut, count, order = PARTS[part]
        ref = region(held(part, phase, step), first, count)
        index = part * 10 + phase * 3 + step % 4 if step else part * 10
        return remote(ref, ref, sib_s.at[index], sib_r.at[0], sibling)

    def ring_start(phase, half):
        for part in range(3):
            for copy in ring_copies(part, phase, half):
                copy.start()

    def ring_wait(phase, half):
        for part in range(3):
            for copy in ring_copies(part, phase, half):
                copy.wait_recv()

    def sib_start(phase, steps):
        for part in range(3):
            for step in steps:
                sib_copy(part, phase, step).start()

    def ring_step(index):
        phase, half = divmod(index, 2)
        ring_wait(phase, half)
        if half == 0:
            ring_start(phase, 1)
            sib_start(phase, (-1, 1))
        else:
            if phase < 2:
                ring_start(phase + 1, 0)
            sib_start(phase, (2,))

    slots[member] = stage[member]
    for copy in group_copies:
        copy.wait_recv()
    whole = jnp.concatenate([slots[m].astype(jnp.float32)[0:98] for m in range(8)], axis=0)
    wf[lax.rem(pos["x"], 2), pos["y"], pos["z"], core, pos["x"] // 2] = whole.astype(jnp.bfloat16)
    ring_start(0, 0)
    sib_start(0, (0,))

    for copy in halo_copies:
        copy.wait_recv()
    zero = jnp.float32(0)
    for a in range(2):
        inside = (row > 0) if a == 0 else (row < 7)
        ext[33 * a] = jnp.where(inside, halo_row[a].astype(jnp.float32), zero).astype(jnp.bfloat16)
        for b in range(2):
            inner = inside & ((col > 0) if b == 0 else (col < 15))
            corner = halo_corner[a, b].astype(jnp.float32)
            cell = corner[15:16] if b == 0 else corner[0:1]
            place = 7 if a == 0 else 40
            side[b, place : place + 1, :] = jnp.where(inner, cell, zero)
    for b in range(2):
        inside = (col > 0) if b == 0 else (col < 15)
        side[b, 8:40, :] = jnp.where(inside, halo_col[b].astype(jnp.float32), zero)
    ext[1:33] = feat[...]
    place = lax.broadcasted_iota(jnp.int32, (32, CH), 0)

    def tap_row(i, carry):
        centre = ext[i].astype(jnp.float32)
        left = jnp.where(place == 0, side[0, pl.ds(7 + i, 1), :], pltpu.roll(centre, 1, 0))
        right = jnp.where(place == 31, side[1, pl.ds(7 + i, 1), :], pltpu.roll(centre, 31, 0))
        taps[i, :, 0:256] = left.astype(jnp.bfloat16)
        taps[i, :, 256:512] = ext[i]
        taps[i, :, 512:768] = right.astype(jnp.bfloat16)
        return carry

    lax.fori_loop(0, 34, tap_row, 0)

    def conv_rows(i, carry):
        first = i * 8
        value = jnp.zeros((256, CH), jnp.float32)
        for a in range(3):
            value = value + dot(taps[pl.ds(first + a, 8)].reshape(256, 768), conv_w[a])
        neck[pl.ds(pl.multiple_of(i * 256, 256), 256), :] = value.astype(jnp.bfloat16)
        return carry

    lax.fori_loop(0, 4, conv_rows, 0)

    lane = lax.broadcasted_iota(jnp.int32, (ROIS, 128), 1)
    angle_hot = jnp.where(lane == meta[:, 1:2].astype(jnp.int32), 1.0, 0.0).astype(jnp.bfloat16)
    base = meta[:, 0:1]
    cell_lane = lax.broadcasted_iota(jnp.int32, (ROIS, CELLS), 1)

    def sample(k, carry):
        cells = (dot(angle_hot, table[k]) + base).astype(jnp.int32)
        for j in range(POOL):
            hot = jnp.where(cell_lane == cells[:, j : j + 1], 1.0, 0.0).astype(jnp.bfloat16)
            x[k, :, 256 * j : 256 * j + 256] = dot(hot, neck[...]).astype(jnp.bfloat16)
        for index in range(4):

            @pl.when(k == index)
            def _():
                ring_step(index)

        return carry

    lax.fori_loop(0, POOL, sample, 0)
    hot_t = jnp.where(
        lax.broadcasted_iota(jnp.int32, (128, ROIS), 0) == meta_t[1:2, :].astype(jnp.int32), 1.0, 0.0
    ).astype(jnp.bfloat16)
    cells_t[...] = (dot(table_t[...], hot_t) + meta_t[0:1, :]).astype(jnp.int32)
    ring_step(4)
    ring_step(5)
    for copy in group_copies + halo_copies:
        copy.wait_send()
    for part in range(3):
        for phase in range(3):
            for half in range(2):
                for copy in ring_copies(part, phase, half):
                    copy.wait_send()
            for step in (0, -1, 1, 2) if phase == 0 else (-1, 1, 2):
                sib_copy(part, phase, step).wait_send()
    other_core = wf.at[:, :, :, 1 - core]
    pltpu.make_async_copy(other_core, other_core, sib_r.at[0]).wait()

    flat = wf.reshape(8, GROUP * 16, 128)

    def weight(first, count, pieces=range(8)):
        return jnp.concatenate([flat[m, pl.ds(first, count), :] for m in pieces], axis=1)

    pre1[...] = jnp.zeros_like(pre1)

    def forward(k, carry):
        first = pl.multiple_of(k * SPAN, SPAN)
        for n in range(4):
            pre1[:, 256 * n : 256 * n + 256] += dot(x[k], weight(first, SPAN, (2 * n, 2 * n + 1)))
        return carry

    lax.fori_loop(0, POOL, forward, 0)

    def activate(pre, gp, hid):
        def some(i, carry):
            rows = pl.ds(pl.multiple_of(i * 32, 32), 32)
            value = pre[rows, :]
            phi = erf_parts(value)
            hid[rows, :] = (value * phi).astype(jnp.bfloat16)
            gp[rows, :] = slope(value, phi)
            return carry

        lax.fori_loop(0, ROIS // 32, some, 0)

    activate(pre1, gp1, hid1)
    for n in range(4):
        pre2[:, 256 * n : 256 * n + 256] = dot(hid1[...], w2[:, 256 * n : 256 * n + 256])
    hid2 = dpre1
    activate(pre2, gp2, hid2)
    z = dot(hid2[...], wo[...])
    label = meta[:, 2:3].astype(jnp.int32)
    live = meta[:, 3:4]
    onehot = jnp.where(lane == label, 1.0, 0.0)
    foreground = jnp.where(label < CLASSES, 1.0, 0.0)
    dlogit = 1.0 / (1.0 + jnp.exp(-(z + prior_logit))) - onehot
    dbox = jnp.clip(z - meta[...], -1.0, 1.0) * foreground
    dz = jnp.where(lane < CLASSES, dlogit, jnp.where(lane < OUTS, dbox, 0.0))
    dz = jnp.where(live > 0.5, dz, 0.0).astype(jnp.bfloat16)
    for n in range(4):
        cols = slice(256 * n, 256 * n + 256)
        dpre2[:, cols] = (dot_nt(dz, wo[cols, :]) * gp2[:, cols]).astype(jnp.bfloat16)

    mine = pl.multiple_of(core * 512, 512)
    theirs = pl.multiple_of(512 - core * 512, 512)
    for start, out in ((theirs, send0), (mine, keep)):
        hid1_half = hid1[:, pl.ds(start, 512)]
        for n in range(4):
            cols = slice(256 * n, 256 * n + 256)
            out[:, cols] = dot_tn(hid1_half, dpre2[:, cols]).astype(out.dtype)
        out[:, HID:] = dot_tn(hid2[:, pl.ds(start, 512)], dz).astype(out.dtype)
        if out is send0:
            remote(send0, recv0, red_s.at[0], red_r.at[0], sibling).start()

    for n in range(4):
        cols = slice(256 * n, 256 * n + 256)
        dpre1[:, cols] = (dot_nt(dpre2[...], w2[cols, :]) * gp1[:, cols]).astype(jnp.bfloat16)

    def order(part, level):
        return PARTS[part][3][level]

    def spot(axis, step):
        return lax.rem(pos[axis] + (step + 4), 4)

    def cols_of(part):
        return pl.ds(COLS * part, COLS)

    def scatter_copies(level, src, dst, rows, sems):
        copies = []
        for part in range(3):
            axis = order(part, level)
            for step in (1, 2, 3):
                piece = src.at[part, pl.ds(pl.multiple_of(spot(axis, step) * rows, rows), rows)]
                sem = sems + part * 3 + step - 1
                copies.append(
                    remote(piece, dst.at[part, step - 1], red_s.at[sem], red_r.at[sem], device(axis, step))
                )
        return copies

    def share_copies(sems):
        copies = []
        for part in range(3):
            axis = order(part, 2)
            for step in (1, 2, 3):
                sem = sems + part * 3 + step - 1
                spot_ref = recv3.at[part, pos[axis]]
                copies.append(remote(spot_ref, spot_ref, red_s.at[sem], red_r.at[sem], device(axis, step)))
        return copies

    def place_of(part, level):
        first = core * 512 + pos[order(part, 0)] * 128
        if level == 1:
            return pl.ds(pl.multiple_of(first + pos[order(part, 1)] * 32, 32), 32)
        return pl.ds(pl.multiple_of(first, 128), 128)

    def spread_copies(level, sems):
        copies = []
        for part in range(3):
            axis = order(part, level)
            for step in (1, 2, 3):
                sem = sems + part * 3 + step - 1
                ref = total.at[place_of(part, level), cols_of(part)]
                copies.append(remote(ref, ref, red_s.at[sem], red_r.at[sem], device(axis, step)))
        return copies

    copy0 = lambda: [remote(send0, recv0, red_s.at[0], red_r.at[0], sibling)]
    copy1 = lambda: scatter_copies(0, send1, recv1, 128, 1)
    copy2 = lambda: scatter_copies(1, send2, recv2, 32, 10)
    copy3 = lambda: share_copies(19)
    copy4 = lambda: spread_copies(1, 28)
    copy5 = lambda: spread_copies(0, 37)

    def copy6():
        ref = total.at[pl.ds(mine, 512)]
        return [remote(ref, ref, red_s.at[46], red_r.at[46], sibling)]

    def start(copies):
        for copy in copies:
            copy.start()

    def wait(copies):
        for copy in copies:
            copy.wait_recv()

    def reduce_step(index):
        if index == 0:
            wait(copy0())
            for part in range(3):
                cols = slice(COLS * part, COLS * part + COLS)

                def some(i, carry):
                    rows = pl.ds(pl.multiple_of(i * 64, 64), 64)
                    value = keep[rows, cols] + recv0[rows, cols].astype(jnp.float32)
                    keep[rows, cols] = value
                    send1[part, rows, :] = value.astype(jnp.bfloat16)
                    return carry

                lax.fori_loop(0, 8, some, 0)
            start(copy1())
        elif index == 1:
            wait(copy1())
            for part in range(3):
                cols = slice(COLS * part, COLS * part + COLS)
                own = pl.ds(pl.multiple_of(pos[order(part, 0)] * 128, 128), 128)
                value = keep[own, cols]
                for step in range(3):
                    value = value + recv1[part, step].astype(jnp.float32)
                keep1[part] = value
                send2[part] = value.astype(jnp.bfloat16)
            start(copy2())
        elif index == 2:
            wait(copy2())
            for part in range(3):
                own = pl.ds(pl.multiple_of(pos[order(part, 1)] * 32, 32), 32)
                value = keep1[part, own, :]
                for step in range(3):
                    value = value + recv2[part, step].astype(jnp.float32)
                recv3[part, pos[order(part, 2)]] = value.astype(jnp.bfloat16)
            start(copy3())
        elif index == 3:
            wait_share()
            for part in range(3):
                value = recv3[part, 0].astype(jnp.float32)
                for step in range(1, 4):
                    value = value + recv3[part, step].astype(jnp.float32)
                cols = slice(COLS * part, COLS * part + COLS)
                total[place_of(part, 1), cols] = value.astype(jnp.bfloat16)
            start(copy4())
        elif index == 4:
            wait(copy4())
            start(copy5())
        elif index == 5:
            wait(copy5())
            start(copy6())

    def wait_share():
        wait(copy3())

    feat_grad[...] = jnp.zeros_like(feat_grad)
    cell_row = lax.broadcasted_iota(jnp.int32, (256, ROIS), 0)

    def backward(k, carry):
        for j in range(POOL):
            first = pl.multiple_of(k * SPAN + 256 * j, 256)
            dxs[256 * j : 256 * j + 256, :] = dot_nt(dpre1[...], weight(first, 256)).astype(jnp.bfloat16)
        for q in range(4):
            for j in range(POOL):
                cells = cells_t[pl.ds(k * POOL + j, 1), :] - 256 * q
                x[q, :, 256 * j : 256 * j + 256] = jnp.where(cell_row == cells, 1.0, 0.0).astype(jnp.bfloat16)
            feat_grad[256 * q : 256 * q + 256, :] += dot(x[q], dxs[...])
        for index in range(6):

            @pl.when(k == index)
            def _():
                reduce_step(index)

        return carry

    lax.fori_loop(0, POOL, backward, 0)
    wait(copy6())
    for make in (copy0, copy1, copy2, copy3, copy4, copy5, copy6):
        for copy in make():
            copy.wait_send()


def on_device(
    features,
    conv_weight,
    first_weight,
    second_weight,
    out_weight,
    roi_count,
    roi_row,
    roi_col,
    roi_angle,
    roi_label,
    roi_target,
):
    f32, bf16 = jnp.float32, jnp.bfloat16
    shift_rows, shift_cols = offset_tables(POOL, ANGLES)
    shift = (shift_rows * 32 + shift_cols).astype(np.float32)
    table = np.zeros((POOL, 128, 128), np.float32)
    table[:, :ANGLES, :POOL] = shift.reshape(ANGLES, POOL, POOL).transpose(1, 0, 2)
    table_t = np.zeros((64, 128), np.float32)
    table_t[:SAMPLES, :ANGLES] = shift.T
    live = jnp.arange(ROIS, dtype=jnp.int32) < roi_count[0]
    facts = [(roi_row * 32 + roi_col), roi_angle, roi_label, live]
    facts = [fact.astype(f32) for fact in facts]
    meta = jnp.concatenate(
        [
            jnp.stack(facts, axis=1),
            jnp.zeros((ROIS, CLASSES - 4), f32),
            roi_target.astype(f32),
            jnp.zeros((ROIS, 128 - OUTS), f32),
        ],
        axis=1,
    )
    meta_t = jnp.stack(facts[:2] + [jnp.zeros((ROIS,), f32)] * 6, axis=0)
    edge_cols = jnp.stack([features[:, 0], features[:, 31]])
    out_wide = jnp.pad(out_weight, ((0, 0), (0, 128 - OUTS)))

    vmem = pl.BlockSpec(memory_space=pltpu.VMEM)
    dma = pltpu.SemaphoreType.DMA
    neck, feat_grad, total = pl.pallas_call(
        kernel,
        out_shape=(
            jax.ShapeDtypeStruct((CELLS, CH), bf16),
            jax.ShapeDtypeStruct((CELLS, CH), f32),
            jax.ShapeDtypeStruct((HID, WIDE), bf16),
        ),
        in_specs=[vmem] * 10,
        out_specs=(vmem, vmem, vmem),
        scratch_shapes=[
            pltpu.VMEM((2, 4, 4, 2, 2, GROUP, 128), bf16),
            pltpu.VMEM((8, 112, 128), bf16),
            pltpu.VMEM((8, 112, 128), bf16),
            pltpu.VMEM((2, 32, CH), bf16),
            pltpu.VMEM((2, 32, CH), bf16),
            pltpu.VMEM((2, 2, 16, CH), bf16),
            pltpu.VMEM((2, 48, CH), f32),
            pltpu.VMEM((34, 32, CH), bf16),
            pltpu.VMEM((34, 32, 3 * CH), bf16),
            pltpu.VMEM((POOL, ROIS, SPAN), bf16),
            pltpu.VMEM((64, ROIS), jnp.int32),
            pltpu.VMEM((ROIS, HID), f32),
            pltpu.VMEM((ROIS, HID), f32),
            pltpu.VMEM((ROIS, HID), f32),
            pltpu.VMEM((ROIS, HID), f32),
            pltpu.VMEM((ROIS, HID), bf16),
            pltpu.VMEM((ROIS, HID), bf16),
            pltpu.VMEM((ROIS, HID), bf16),
            pltpu.VMEM((SPAN, CH), bf16),
            pltpu.VMEM((512, WIDE), f32),
            pltpu.VMEM((512, WIDE), bf16),
            pltpu.VMEM((512, WIDE), bf16),
            pltpu.VMEM((3, 512, COLS), bf16),
            pltpu.VMEM((3, 3, 128, COLS), bf16),
            pltpu.VMEM((3, 128, COLS), f32),
            pltpu.VMEM((3, 128, COLS), bf16),
            pltpu.VMEM((3, 3, 32, COLS), bf16),
            pltpu.VMEM((3, 32, COLS), f32),
            pltpu.VMEM((3, 4, 32, COLS), bf16),
            dma((8,)),
            dma((8,)),
            dma((7,)),
            dma((7,)),
            dma((36,)),
            dma((36,)),
            dma((30,)),
            dma((1,)),
            dma((47,)),
            dma((47,)),
        ],
        compiler_params=pltpu.CompilerParams(
            collective_id=0, has_side_effects=True, vmem_limit_bytes=60 * 2**20
        ),
    )(
        features,
        edge_cols,
        conv_weight.reshape(3, 3 * CH, CH),
        first_weight,
        second_weight,
        out_wide,
        meta,
        meta_t,
        jnp.asarray(table, bf16),
        jnp.asarray(table_t, bf16),
    )
    return (
        neck.reshape(32, 32, CH),
        feat_grad.reshape(32, 32, CH),
        total[:, :HID].astype(f32),
        total[:, HID : HID + OUTS].astype(f32),
    )


def solution(mesh):
    in_specs = (
        P("row", "col", None),
        P(),
        P(("row", "col"), None),
        P(),
        P(),
        P(("row", "col")),
        P(("row", "col")),
        P(("row", "col")),
        P(("row", "col")),
        P(("row", "col")),
        P(("row", "col"), None),
    )
    out_specs = (P("row", "col", None), P("row", "col", None), P(), P())
    return jax.shard_map(
        on_device, mesh=mesh, in_specs=in_specs, out_specs=out_specs, check_vma=False
    )
```

```python
import heapq
import math

import jax
import jax.numpy as jnp
import numpy as np
from jax import lax
from jax.experimental import pallas as pl
from jax.experimental.pallas import tpu as pltpu
from jax.sharding import PartitionSpec as P

POOL = 7
ANGLES = 8
CLASSES = 37
OUTS = 42
HID = 1024
CH = 256
CELLS = 1024
ROIS = 256
SAMPLES = POOL * POOL
GROUP = 784
SPAN = POOL * CH
WIDE = HID + 128
COLS = WIDE // 3
MESH = pl.DeviceIdType.MESH
SLOTS = (0, 5, 7, 9, 11)

prior_logit = -4.59512

PARTS = (
    (0, 128, 256, "xyz"),
    (256, 128, 256, "yzx"),
    (512, 144, 272, "zxy"),
)


LINK = 46.5e3
DELAY = 2.2


def arrivals():
    free, events, got, order, count = {}, [], set(), [], 0
    waiting = {axis: [] for axis in "xyz"}
    opened = set()

    def push(now, axis, way, size, item):
        nonlocal count
        end = max(now, free.get((axis, way), 0.0)) + size / LINK
        free[(axis, way)] = end
        count += 1
        heapq.heappush(events, (end + DELAY, count, item))

    def send(now, item):
        part, phase, key, half, way = item
        first, cut, rows, axes = PARTS[part]
        part_rows = rows if half == 0 else cut if way == 0 else rows - cut
        push(now, axes[phase], way, part_rows * 256 * (4 if phase == 2 else 1), item)

    for item in first_sends():
        send(0.0, item)
    while events:
        now, _, item = heapq.heappop(events)
        got.add(item)
        order.append((now, item))
        for after in follow(item, got, waiting, opened):
            send(now, after)
    return order


def both(part, phase, key):
    return [(part, phase, key, 0, 0), (part, phase, key, 0, 1)]


def first_sends():
    return [item for phase in (0, 1) for part in range(3) for item in both(part, phase, 0)]


def follow(item, got, waiting, opened):
    part, phase, key, half, way = item
    sends = [(part, phase, key, 1, way)] if half == 0 else []
    lines = []
    if phase == 0:
        if half == 0:
            sends += both(part, 1, -1 if way == 0 else 1)
        elif (part, 0, 0, 1, 1 - way) in got:
            sends += both(part, 1, 2)
            lines.append(0)
    elif phase == 1:
        offsets = (0, -1, 1, 2)
        if half == 0 and all((part, 1, k, 0, way) in got for k in offsets):
            lines.append(-1 if way == 0 else 1)
        if half == 1 and all((part, 1, k, 1, w) in got for k in offsets for w in (0, 1)):
            lines.append(2)
    for line in lines:
        axis = PARTS[part][3][2]
        if axis in opened:
            sends += both(part, 2, line)
        else:
            waiting[axis].append((part, line))
    if phase == 1:
        axis = PARTS[part][3][1]
        if axis not in opened and all((part, 1, k, 0, w) in got for k in (0, -1, 1, 2) for w in (0, 1)):
            opened.add(axis)
            for other, line in waiting[axis]:
                sends += both(other, 2, line)
    return sends


def offset_tables(pool, angles):
    turn = np.arange(angles) * math.pi / angles
    along = np.arange(pool) - pool // 2
    down = (along[:, None] * np.ones((1, pool))).reshape(1, -1)
    across = (np.ones((pool, 1)) * along[None, :]).reshape(1, -1)
    cosine = np.cos(turn)[:, None]
    sine = np.sin(turn)[:, None]
    shift_rows = np.floor(down * cosine - across * sine + 0.5).astype(np.int32)
    shift_cols = np.floor(down * sine + across * cosine + 0.5).astype(np.int32)
    return (shift_rows, shift_cols)


def erf_parts(value):
    return 0.5 * (1.0 + lax.erf(value * math.sqrt(0.5)))


def slope(value, phi):
    return phi + value * jnp.exp(-0.5 * value * value) * (1.0 / math.sqrt(2.0 * math.pi))


def dot(a, b):
    return jnp.dot(a, b, preferred_element_type=jnp.float32)


def dot_nt(a, b):
    return lax.dot_general(a, b, (((1,), (1,)), ((), ())), preferred_element_type=jnp.float32)


def dot_tn(a, b):
    return lax.dot_general(a, b, (((0,), (0,)), ((), ())), preferred_element_type=jnp.float32)


def kernel(
    feat,
    conv_hbm,
    shard,
    w2_hbm,
    out_w,
    count,
    roi_row,
    roi_col,
    roi_angle,
    roi_label,
    roi_target,
    table,
    table_t,
    neck_hbm,
    grad_hbm,
    total_hbm,
    neck,
    feat_grad,
    total,
    wf,
    conv_w,
    w2,
    wo,
    facts,
    meta,
    edges,
    edge_cols,
    stage,
    slots,
    halo_row,
    halo_col,
    halo_corner,
    side,
    ext,
    taps,
    xg,
    xt,
    window,
    cells_all,
    cells_t,
    pre1,
    gp1,
    gp2,
    hid1,
    dpre2,
    dpre1,
    dxs,
    keep,
    send0,
    recv0,
    send1,
    recv1,
    keep1,
    send2,
    recv2,
    recv3,
    halo_s,
    halo_r,
    group_s,
    group_r,
    ring_s,
    ring_r,
    sib_s,
    sib_r,
    red_s,
    red_r,
    in_s,
    out_s,
):
    row = lax.axis_index("row")
    col = lax.axis_index("col")
    pos = {"x": col // 4, "y": lax.rem(col, 4), "z": row // 2}
    core = lax.rem(row, 2)

    def device(axis, step):
        at = dict(pos)
        at[axis] = lax.rem(pos[axis] + (step + 4), 4)
        return (at["z"] * 2 + core, at["x"] * 4 + at["y"])

    sibling = (row + 1 - 2 * core, col)
    member = lax.rem(col, 8)

    def group_device(step):
        return (row, col - member + lax.rem(member + step, 8))

    around = [(a, b) for a in (-1, 0, 1) for b in (-1, 0, 1) if (a, b) != (0, 0)]

    def halo_device(a, b):
        return (lax.rem(row + a + 8, 8), lax.rem(col + b + 16, 16))

    barrier = pltpu.get_barrier_semaphore()
    partners = [sibling] + [device(axis, step) for axis in "xz" for step in (1, 3)]
    partners += [group_device(step) for step in range(1, 8)]
    partners += [halo_device(a, b) for a, b in around]
    for partner in partners:
        pl.semaphore_signal(barrier, inc=1, device_id=partner, device_id_type=MESH)
    pl.semaphore_wait(barrier, len(partners))

    def remote(src, dst, send_sem, recv_sem, target):
        return pltpu.make_async_remote_copy(
            src_ref=src,
            dst_ref=dst,
            send_sem=send_sem,
            recv_sem=recv_sem,
            device_id=target,
            device_id_type=MESH,
        )

    loads = [
        pltpu.make_async_copy(conv_hbm, conv_w, in_s.at[0]),
        pltpu.make_async_copy(w2_hbm, w2, in_s.at[1]),
    ]
    stores = [
        pltpu.make_async_copy(neck, neck_hbm, out_s.at[0]),
        pltpu.make_async_copy(feat_grad, grad_hbm, out_s.at[1]),
        pltpu.make_async_copy(total, total_hbm, out_s.at[2]),
    ]
    for load in loads:
        load.start()

    def group_copy(step):
        other = lax.rem(member + step, 8)
        return remote(
            stage.at[other], slots.at[member], group_s.at[step - 1], group_r.at[step - 1], group_device(step)
        )

    for m in range(8):
        stage[m, 0:98, :] = shard[:, 128 * m : 128 * m + 128]
    group_copies = [group_copy(step) for step in range(1, 8)]
    for copy in group_copies:
        copy.start()

    for i in range(32):
        cells_in_row = feat[i].astype(jnp.float32)
        edges[0, i : i + 1, :] = cells_in_row[0:1]
        edges[1, i : i + 1, :] = cells_in_row[31:32]
    edge_cols[...] = edges[...].astype(jnp.bfloat16)

    def halo_copy(index):
        a, b = around[index]
        if b == 0:
            src, dst = feat.at[0 if a < 0 else 31], halo_row.at[0 if a > 0 else 1]
        elif a == 0:
            src, dst = edge_cols.at[0 if b < 0 else 1], halo_col.at[0 if b > 0 else 1]
        else:
            src = feat.at[0 if a < 0 else 31, pl.ds(0 if b < 0 else 16, 16)]
            dst = halo_corner.at[0 if a > 0 else 1, 0 if b > 0 else 1]
        return remote(src, dst, halo_s.at[index], halo_r.at[index], halo_device(a, b))

    halo_copies = [halo_copy(index) for index in range(8)]
    for copy in halo_copies:
        copy.start()

    def region(at, first, count):
        def one(axis):
            return slice(None) if at[axis] is None else at[axis]

        if at["x"] is None:
            low, high = slice(None), slice(None)
        else:
            low, high = lax.rem(at["x"], 2), at["x"] // 2
        return wf.at[low, one("y"), one("z"), core, high, pl.ds(first, count)]

    def spot(axis, step):
        return lax.rem(pos[axis] + (step + 4), 4)

    def item_copy(item):
        part, phase, key, half, way = item
        first, cut, rows, axes = PARTS[part]
        at = dict(pos)
        if phase == 1:
            at[axes[0]] = spot(axes[0], key)
        if phase == 2:
            at[axes[0]] = None
            at[axes[1]] = spot(axes[1], key)
        axis = axes[phase]
        if half == 1:
            at[axis] = spot(axis, -1 if way == 0 else 1)
            first, rows = (first, cut) if way == 0 else (first + cut, rows - cut)
        ref = region(at, first, rows)
        sem = part * 36 + (phase * 16 - 12 if phase else 0) + (key % 4) * 4 + half * 2 + way
        return remote(ref, ref, ring_s.at[sem], ring_r.at[sem], device(axis, 1 if way == 0 else -1))

    def line_copy(part, near, far):
        first, cut, rows, axes = PARTS[part]
        at = {axes[0]: None, axes[1]: spot(axes[1], near), axes[2]: spot(axes[2], far)}
        ref = region(at, first, rows)
        index = part * 4 + far % 4
        return remote(ref, ref, sib_s.at[index * 4 + near % 4], sib_r.at[index], sibling)

    def line_wait(part, far):
        first, cut, rows, axes = PARTS[part]
        at = {axes[0]: None, axes[1]: None, axes[2]: spot(axes[2], far)}
        ref = region(at, first, rows)
        pltpu.make_async_copy(ref, ref, sib_r.at[part * 4 + far % 4]).wait()

    got, waiting, opened = set(), {axis: [] for axis in "xyz"}, set()

    def arrive(item):
        item_copy(item).wait_recv()
        got.add(item)
        for after in follow(item, got, waiting, opened):
            item_copy(after).start()
        part, phase, key, half, way = item
        offsets = (0, -1, 1, 2)
        if phase == 0 and half == 1 and (part, 0, 0, 1, 1 - way) in got:
            line_copy(part, 0, 0).start()
        if phase == 1 and half == 0 and all((part, 1, k, 0, way) in got for k in offsets):
            line_copy(part, -1 if way == 0 else 1, 0).start()
        if phase == 1 and half == 1 and all((part, 1, k, 1, w) in got for k in offsets for w in (0, 1)):
            line_copy(part, 2, 0).start()
        if phase == 2 and half == 0:
            line_copy(part, key, -1 if way == 0 else 1).start()
        if phase == 2 and half == 1 and (part, 2, key, 1, 1 - way) in got:
            line_copy(part, key, 2).start()

    facts[...] = jnp.zeros_like(facts)
    position = lax.broadcasted_iota(jnp.int32, (1, ROIS), 1)
    angle_row = roi_angle[...].reshape(1, ROIS)
    base_row = roi_row[...].reshape(1, ROIS) * 32 + roi_col[...].reshape(1, ROIS)
    facts[0:1, :] = base_row.astype(jnp.float32)
    facts[1:2, :] = angle_row.astype(jnp.float32)
    facts[2:3, :] = roi_label[...].reshape(1, ROIS).astype(jnp.float32)
    facts[3:4, :] = jnp.where(position < count[0], 1.0, 0.0)
    facts[CLASSES:OUTS, :] = roi_target[...].astype(jnp.float32)
    meta[...] = facts[...].T
    wo[...] = jnp.zeros_like(wo)
    wo[0:OUTS, :] = out_w[...]
    lane = lax.broadcasted_iota(jnp.int32, (ROIS, 128), 1)
    angle_hot = jnp.where(lane == meta[:, 1:2].astype(jnp.int32), 1.0, 0.0).astype(jnp.bfloat16)
    cells_all[...] = dot(angle_hot, table[...]) + meta[:, 0:1]
    hot_t = jnp.where(lax.broadcasted_iota(jnp.int32, (128, ROIS), 0) == angle_row, 1.0, 0.0)
    cells_t[...] = dot(table_t[...], hot_t.astype(jnp.bfloat16)).astype(jnp.int32) + base_row

    slots[member] = stage[member]
    for copy in group_copies:
        copy.wait_recv()
    whole = jnp.concatenate([slots[m].astype(jnp.float32)[0:98] for m in range(8)], axis=0)
    wf[lax.rem(pos["x"], 2), pos["y"], pos["z"], core, pos["x"] // 2] = whole.astype(jnp.bfloat16)
    for item in first_sends():
        item_copy(item).start()

    loads[0].wait()
    for copy in halo_copies:
        copy.wait_recv()
    zero = jnp.float32(0)
    for a in range(2):
        inside = (row > 0) if a == 0 else (row < 7)
        ext[33 * a] = jnp.where(inside, halo_row[a].astype(jnp.float32), zero).astype(jnp.bfloat16)
        for b in range(2):
            inner = inside & ((col > 0) if b == 0 else (col < 15))
            corner = halo_corner[a, b].astype(jnp.float32)
            cell = corner[15:16] if b == 0 else corner[0:1]
            place = 7 if a == 0 else 40
            side[b, place : place + 1, :] = jnp.where(inner, cell, zero)
    for b in range(2):
        inside = (col > 0) if b == 0 else (col < 15)
        side[b, 8:40, :] = jnp.where(inside, halo_col[b].astype(jnp.float32), zero)
    ext[1:33] = feat[...]
    place = lax.broadcasted_iota(jnp.int32, (32, CH), 0)

    def tap_row(i, carry):
        centre = ext[i].astype(jnp.float32)
        left = jnp.where(place == 0, side[0, pl.ds(7 + i, 1), :], pltpu.roll(centre, 1, 0))
        right = jnp.where(place == 31, side[1, pl.ds(7 + i, 1), :], pltpu.roll(centre, 31, 0))
        taps[i, :, 0:256] = left.astype(jnp.bfloat16)
        taps[i, :, 256:512] = ext[i]
        taps[i, :, 512:768] = right.astype(jnp.bfloat16)
        return carry

    lax.fori_loop(0, 34, tap_row, 0)

    def conv_rows(i, carry):
        first = i * 8
        value = jnp.zeros((256, CH), jnp.float32)
        for a in range(3):
            value = value + dot(taps[pl.ds(first + a, 8)].reshape(256, 768), conv_w[a])
        neck[pl.ds(pl.multiple_of(i * 256, 256), 256), :] = value.astype(jnp.bfloat16)
        return carry

    lax.fori_loop(0, 4, conv_rows, 0)
    stores[0].start()

    cell_lane = lax.broadcasted_iota(jnp.int32, (ROIS, CELLS), 1)

    def picked(cells, j):
        hot = jnp.where(cell_lane == cells[:, j : j + 1].astype(jnp.int32), 1.0, 0.0).astype(jnp.bfloat16)
        return dot(hot, neck[...])

    window[:, 0:256] = picked(cells_all[...], 0)
    xt[...] = jnp.zeros_like(xt)
    group_lane = lax.broadcasted_iota(jnp.int32, (ROIS, CH), 1) // 16

    def sample(g):
        cells = pltpu.roll(cells_all[...], 127 - 3 * g, 1)
        for j in range(3):
            window[:, 256 + 256 * j : 512 + 256 * j] = picked(cells, j)
        last = window[:, 768:1024]
        xt[...] = jnp.where(group_lane == g, last.astype(jnp.bfloat16), xt[...])
        far = g // 8
        shift = 16 * lax.rem(g, 8)
        back = lax.rem(128 - shift, 128)
        for i in range(6):
            low = pltpu.roll(window[:, pl.ds(pl.multiple_of(128 * (far + i), 128), 128)], back, 1)
            high = pltpu.roll(window[:, pl.ds(pl.multiple_of(128 * (far + i + 1), 128), 128)], back, 1)
            place = pl.ds(pl.multiple_of(768 * lax.rem(g, 2) + 128 * i, 128), 128)
            xg[g // 2, :, place] = jnp.where(lane < 128 - shift, low, high).astype(jnp.bfloat16)
        window[:, 0:256] = last

    def entries(z, c, high, first):
        return xg[z * 2 + c, :, pl.ds(pl.multiple_of(768 * high + first, 256), 256)]

    def product(part, far):
        axis = PARTS[part][3][2]
        here = spot(axis, far)
        line_wait(part, far)
        if axis == "z":
            pairs = [(c, high) for c in range(2) for high in range(2)]
            left = jnp.concatenate([entries(here, c, high, 0) for c, high in pairs], axis=1)
            for n in range(4):
                low, y = n // 2, 2 * (n % 2)
                halves = [
                    jnp.concatenate([wf[low, y + i, here, c, high, 0:256, :] for c, high in pairs], axis=0)
                    for i in range(2)
                ]
                pre1[:, 256 * n : 256 * n + 256] += dot(left, jnp.concatenate(halves, axis=1))
        elif axis == "x":
            low, high = lax.rem(here, 2), here // 2
            for z in range(0, 4, 2):
                pairs = [(z + i, c) for i in range(2) for c in range(2)]
                left = jnp.concatenate([entries(a, c, high, 256) for a, c in pairs], axis=1)
                for n in range(2):
                    halves = [
                        jnp.concatenate([wf[low, 2 * n + i, a, c, high, 256:512, :] for a, c in pairs], axis=0)
                        for i in range(2)
                    ]
                    cols = pl.ds(pl.multiple_of(512 * low + 256 * n, 256), 256)
                    pre1[:, cols] += dot(left, jnp.concatenate(halves, axis=1))
        else:

            def some(z, carry):
                pairs = [(c, high) for c in range(2) for high in range(2)]
                left = jnp.concatenate([entries(z, c, high, 512) for c, high in pairs], axis=1)
                halves = [
                    jnp.concatenate([wf[low, here, z, c, high, 512:768, :] for c, high in pairs], axis=0)
                    for low in range(2)
                ]
                add(dot(left, jnp.concatenate(halves, axis=1)))
                return carry

            def add(value):
                for low in range(2):
                    cols = pl.ds(pl.multiple_of(512 * low + 128 * here, 128), 128)
                    pre1[:, cols] += value[:, 128 * low : 128 * low + 128]

            lax.fori_loop(0, 4, some, 0)
            groups = [(z, c, high) for z in range(4) for c in range(2) for high in range(2)]
            halves = [
                jnp.concatenate([wf[low, here, z, c, high, 768:784, :] for z, c, high in groups], axis=0)
                for low in range(2)
            ]
            add(dot(xt[...], jnp.concatenate(halves, axis=1)))

    events = arrivals()
    now = 3.0
    batches = []
    for g in range(16):
        batches.append([])
        while events and events[0][0] <= now + 0.5:
            time, item = events.pop(0)
            now = max(now + 0.05, time)
            batches[-1].append(item)
        now += 1.1
    pre1[...] = jnp.zeros_like(pre1)

    def sample_step(g, carry):
        for index, batch in enumerate(batches):
            if batch:

                @pl.when(g == index)
                def _(batch=batch):
                    for item in batch:
                        arrive(item)

        sample(g)
        return carry

    lax.fori_loop(0, 16, sample_step, 0)
    due = {}
    for time, item in arrivals():
        part, phase, key, half, way = item
        far = 0 if phase < 2 else 2 if half else -1 if way == 0 else 1
        due[(part, far)] = max(due.get((part, far), 0.0), time + 3.0)
    todo = sorted((time, key) for key, time in due.items())
    while todo or events:
        if events and (events[0][0] <= now + 0.3 or not todo):
            time, item = events.pop(0)
            now = max(now + 0.05, time)
            arrive(item)
        elif todo and (todo[0][0] <= now or not events):
            product(*todo.pop(0)[1])
            now += 0.7
        else:
            now = min(events[0][0], todo[0][0])
    for copy in group_copies + halo_copies:
        copy.wait_send()
    for part in range(3):
        for phase in range(3):
            for key in (0, -1, 1, 2) if phase else (0,):
                for half in range(2):
                    for way in range(2):
                        item_copy((part, phase, key, half, way)).wait_send()
        for near in (0, -1, 1, 2):
            for far in (0, -1, 1, 2):
                line_copy(part, near, far).wait_send()
    loads[1].wait()

    flat = wf.reshape(8, GROUP * 16, 128)

    def weight(first, count):
        return jnp.concatenate([flat[m, pl.ds(first, count), :] for m in range(8)], axis=1)

    def activate(pre, hid, gp):
        def some(i, carry):
            rows = pl.ds(pl.multiple_of(i * 32, 32), 32)
            value = pre[rows, :]
            phi = erf_parts(value)
            if hid is not None:
                hid[rows, :] = (value * phi).astype(jnp.bfloat16)
            if gp is not None:
                gp[rows, :] = slope(value, phi)
            return carry

        lax.fori_loop(0, ROIS // 32, some, 0)

    activate(pre1, hid1, None)
    pre2 = window
    for n in range(4):
        pre2[:, 256 * n : 256 * n + 256] = dot(hid1[...], w2[:, 256 * n : 256 * n + 256])
    hid2 = dpre1
    activate(pre2, hid2, gp2)
    z = dot_nt(hid2[...], wo[...])
    label = meta[:, 2:3].astype(jnp.int32)
    live = meta[:, 3:4]
    onehot = jnp.where(lane == label, 1.0, 0.0)
    foreground = jnp.where(label < CLASSES, 1.0, 0.0)
    dlogit = 1.0 / (1.0 + jnp.exp(-(z + prior_logit))) - onehot
    dbox = jnp.clip(z - meta[...], -1.0, 1.0) * foreground
    dz = jnp.where(lane < CLASSES, dlogit, jnp.where(lane < OUTS, dbox, 0.0))
    dz = jnp.where(live > 0.5, dz, 0.0).astype(jnp.bfloat16)
    for n in range(4):
        cols = slice(256 * n, 256 * n + 256)
        dpre2[:, cols] = (dot(dz, wo[:, cols]) * gp2[:, cols]).astype(jnp.bfloat16)

    mine = pl.multiple_of(core * 512, 512)
    theirs = pl.multiple_of(512 - core * 512, 512)

    def half_grad(start, cols):
        if cols.stop <= HID:
            return dot_tn(hid1[:, pl.ds(start, 512)], dpre2[:, cols])
        return jnp.concatenate(
            [
                dot_tn(hid1[:, pl.ds(start, 512)], dpre2[:, cols.start : HID]),
                dot_tn(hid2[:, pl.ds(start, 512)], dz),
            ],
            axis=1,
        )

    def copy0(part):
        return [remote(send0.at[part], recv0.at[part], red_s.at[part], red_r.at[part], sibling)]

    for part in range(3):
        send0[part] = half_grad(theirs, slice(COLS * part, COLS * part + COLS)).astype(jnp.bfloat16)
        copy0(part)[0].start()
    for part in range(3):
        keep[part] = half_grad(mine, slice(COLS * part, COLS * part + COLS))
    activate(pre1, None, gp1)

    for n in range(4):
        cols = slice(256 * n, 256 * n + 256)
        dpre1[:, cols] = (dot_nt(dpre2[...], w2[cols, :]) * gp1[:, cols]).astype(jnp.bfloat16)

    def order(part, level):
        return PARTS[part][3][level]

    def cols_of(part):
        return pl.ds(COLS * part, COLS)

    def scatter_copies(part, level, src, dst, rows, sems):
        copies = []
        axis = order(part, level)
        for step in (1, 3, 2):
            piece = src.at[part, pl.ds(pl.multiple_of(spot(axis, step) * rows, rows), rows)]
            sem = sems + part * 3 + step - 1
            copies.append(remote(piece, dst.at[part, step - 1], red_s.at[sem], red_r.at[sem], device(axis, step)))
        return copies

    def copy1(part):
        return scatter_copies(part, 0, send1, recv1, 128, 3)

    def copy2(part):
        return scatter_copies(part, 1, send2, recv2, 32, 12)

    def copy3(part):
        copies = []
        axis = order(part, 2)
        for step in (1, 3, 2):
            sem = 21 + part * 3 + step - 1
            ref = recv3.at[part, pos[axis]]
            copies.append(remote(ref, ref, red_s.at[sem], red_r.at[sem], device(axis, step)))
        return copies

    def rows_at(part, step):
        return pl.ds(pl.multiple_of(core * 512 + spot(order(part, 0), step) * 128, 128), 128)

    def rows_own(part):
        first = core * 512 + pos[order(part, 0)] * 128 + pos[order(part, 1)] * 32
        return pl.ds(pl.multiple_of(first, 32), 32)

    def spread_copies(part, level, rows, sems):
        copies = []
        axis = order(part, level)
        for step in (1, 3, 2):
            sem = sems + part * 3 + step - 1
            ref = total.at[rows, cols_of(part)]
            copies.append(remote(ref, ref, red_s.at[sem], red_r.at[sem], device(axis, step)))
        return copies

    def copy4(part):
        return spread_copies(part, 1, rows_own(part), 30)

    def copy5(part):
        return spread_copies(part, 0, rows_at(part, 0), 39)

    def copy6(part, step):
        ref = total.at[rows_at(part, step), cols_of(part)]
        return remote(ref, ref, red_s.at[48 + part * 4 + step], red_r.at[48], sibling)

    def start(copies):
        for copy in copies:
            copy.start()

    def wait(copies):
        for copy in copies:
            copy.wait_recv()

    def reduce_step(level, part):
        if level == 0:
            wait(copy0(part))

            def some(i, carry):
                rows = pl.ds(pl.multiple_of(i * 64, 64), 64)
                value = keep[part, rows, :] + recv0[part, rows, :].astype(jnp.float32)
                keep[part, rows, :] = value
                send1[part, rows, :] = value.astype(jnp.bfloat16)
                return carry

            lax.fori_loop(0, 8, some, 0)
            start(copy1(part))
        elif level == 1:
            wait(copy1(part))
            own = pl.ds(pl.multiple_of(pos[order(part, 0)] * 128, 128), 128)
            value = keep[part, own, :]
            for step in range(3):
                value = value + recv1[part, step].astype(jnp.float32)
            keep1[part] = value
            send2[part] = value.astype(jnp.bfloat16)
            start(copy2(part))
        elif level == 2:
            wait(copy2(part))
            own = pl.ds(pl.multiple_of(pos[order(part, 1)] * 32, 32), 32)
            value = keep1[part, own, :]
            for step in range(3):
                value = value + recv2[part, step].astype(jnp.float32)
            recv3[part, pos[order(part, 2)]] = value.astype(jnp.bfloat16)
            start(copy3(part))
        elif level == 3:
            wait(copy3(part))
            value = recv3[part, 0].astype(jnp.float32)
            for step in range(1, 4):
                value = value + recv3[part, step].astype(jnp.float32)
            total[rows_own(part), cols_of(part)] = value.astype(jnp.bfloat16)
            start(copy4(part))
        elif level == 4:
            wait(copy4(part))
            start(copy5(part))
            copy6(part, 0).start()
        elif level == 5:
            for step, copy in zip((1, 3, 2), copy5(part)):
                copy.wait_recv()
                copy6(part, 4 - step).start()

    feat_grad[...] = jnp.zeros_like(feat_grad)
    cell_row = lax.broadcasted_iota(jnp.int32, (256, ROIS), 0)

    def reduce_at(k, slot):
        for level, due_slot in enumerate(SLOTS):
            if due_slot % 2 == slot:

                @pl.when(k == due_slot // 2)
                def _():
                    for part in range(3):
                        reduce_step(level, part)

    def backward(k, carry):
        for j in range(POOL):
            first = pl.multiple_of(k * SPAN + 256 * j, 256)
            dxs[256 * j : 256 * j + 256, :] = dot_nt(dpre1[...], weight(first, 256)).astype(jnp.bfloat16)
        reduce_at(k, 0)
        for q in range(4):
            for j in range(POOL):
                cells = cells_t[pl.ds(k * POOL + j, 1), :] - 256 * q
                hot = jnp.where(cell_row == cells, 1.0, 0.0).astype(jnp.bfloat16)
                xg[q, :, 256 * j : 256 * j + 256] = hot
            feat_grad[256 * q : 256 * q + 256, :] += dot(xg[q], dxs[...])
        reduce_at(k, 1)
        return carry

    lax.fori_loop(0, POOL, backward, 0)
    stores[1].start()
    for part in range(3):
        reduce_step(5, part)
    half_rows = total.at[pl.ds(theirs, 512)]
    pltpu.make_async_copy(half_rows, half_rows, red_r.at[48]).wait()
    stores[2].start()
    for part in range(3):
        for make in (copy0, copy1, copy2, copy3, copy4, copy5):
            for copy in make(part):
                copy.wait_send()
        for step in range(4):
            copy6(part, step).wait_send()
    for store in stores:
        store.wait()


PIECES = 4


def finish(neck_in, grad_in, total_in, neck, feat_grad, second_grad, out_grad, total, wide, turned, cells, grads, loaded, stored):
    rows = HID // PIECES
    copies = []
    for i in range(PIECES):
        part = pl.ds(i * rows, rows)
        for n, (src, held, dst) in enumerate(
            [(total_in, total, None), (grad_in, grads, feat_grad), (neck_in, cells, neck)]
        ):
            load = pltpu.make_async_copy(src.at[part], held.at[part], loaded.at[n, i])
            load.start()
            if dst is not None:
                copies.append((load, pltpu.make_async_copy(held.at[part], dst.at[part], stored.at[n, i])))
            else:
                wide_part = pltpu.make_async_copy(wide.at[part], second_grad.at[part], stored.at[0, i])
                copies.append((load, wide_part))
    last = pltpu.make_async_copy(turned, out_grad, stored.at[0, PIECES])
    for i in range(PIECES):
        part = slice(i * rows, (i + 1) * rows)
        for n in range(3):
            load, store = copies[3 * i + n]
            load.wait()
            if n == 0:
                wide[part, :] = total[part, 0:HID].astype(jnp.float32)
                turned[:, part] = total[part, HID:].astype(jnp.float32).T[0:OUTS]
            store.start()
    last.start()
    for load, store in copies:
        store.wait()
    last.wait()


def on_device(
    features,
    conv_weight,
    first_weight,
    second_weight,
    out_weight,
    roi_count,
    roi_row,
    roi_col,
    roi_angle,
    roi_label,
    roi_target,
):
    f32, bf16 = jnp.float32, jnp.bfloat16
    shift_rows, shift_cols = offset_tables(POOL, ANGLES)
    shift = (shift_rows * 32 + shift_cols).astype(np.float32)
    table = np.zeros((128, 128), np.float32)
    table[:ANGLES, :SAMPLES] = shift
    table_t = np.ascontiguousarray(table.T[:64])

    vmem = pl.BlockSpec(memory_space=pltpu.VMEM)
    hbm = pl.BlockSpec(memory_space=pl.ANY)
    smem = pl.BlockSpec(memory_space=pltpu.SMEM)
    dma = pltpu.SemaphoreType.DMA
    neck, feat_grad, total = pl.pallas_call(
        kernel,
        out_shape=(
            jax.ShapeDtypeStruct((CELLS, CH), bf16),
            jax.ShapeDtypeStruct((CELLS, CH), f32),
            jax.ShapeDtypeStruct((HID, WIDE), bf16),
        ),
        in_specs=[vmem, hbm, vmem, hbm, vmem, smem] + [vmem] * 7,
        out_specs=(hbm, hbm, hbm),
        scratch_shapes=[
            pltpu.VMEM((CELLS, CH), bf16),
            pltpu.VMEM((CELLS, CH), f32),
            pltpu.VMEM((HID, WIDE), bf16),
            pltpu.VMEM((2, 4, 4, 2, 2, GROUP, 128), bf16),
            pltpu.VMEM((3, 3 * CH, CH), bf16),
            pltpu.VMEM((HID, HID), bf16),
            pltpu.VMEM((128, HID), bf16),
            pltpu.VMEM((128, ROIS), f32),
            pltpu.VMEM((ROIS, 128), f32),
            pltpu.VMEM((2, 32, CH), f32),
            pltpu.VMEM((2, 32, CH), bf16),
            pltpu.VMEM((8, 112, 128), bf16),
            pltpu.VMEM((8, 112, 128), bf16),
            pltpu.VMEM((2, 32, CH), bf16),
            pltpu.VMEM((2, 32, CH), bf16),
            pltpu.VMEM((2, 2, 16, CH), bf16),
            pltpu.VMEM((2, 48, CH), f32),
            pltpu.VMEM((34, 32, CH), bf16),
            pltpu.VMEM((34, 32, 3 * CH), bf16),
            pltpu.VMEM((8, ROIS, SPAN), bf16),
            pltpu.VMEM((ROIS, CH), bf16),
            pltpu.VMEM((ROIS, 1024), f32),
            pltpu.VMEM((ROIS, 128), f32),
            pltpu.VMEM((64, ROIS), jnp.int32),
            pltpu.VMEM((ROIS, HID), f32),
            pltpu.VMEM((ROIS, HID), f32),
            pltpu.VMEM((ROIS, HID), f32),
            pltpu.VMEM((ROIS, HID), bf16),
            pltpu.VMEM((ROIS, HID), bf16),
            pltpu.VMEM((ROIS, HID), bf16),
            pltpu.VMEM((SPAN, CH), bf16),
            pltpu.VMEM((3, 512, COLS), f32),
            pltpu.VMEM((3, 512, COLS), bf16),
            pltpu.VMEM((3, 512, COLS), bf16),
            pltpu.VMEM((3, 512, COLS), bf16),
            pltpu.VMEM((3, 3, 128, COLS), bf16),
            pltpu.VMEM((3, 128, COLS), f32),
            pltpu.VMEM((3, 128, COLS), bf16),
            pltpu.VMEM((3, 3, 32, COLS), bf16),
            pltpu.VMEM((3, 4, 32, COLS), bf16),
            dma((8,)),
            dma((8,)),
            dma((7,)),
            dma((7,)),
            dma((108,)),
            dma((108,)),
            dma((48,)),
            dma((12,)),
            dma((60,)),
            dma((49,)),
            dma((2,)),
            dma((3,)),
        ],
        compiler_params=pltpu.CompilerParams(
            collective_id=0, has_side_effects=True, vmem_limit_bytes=60 * 2**20
        ),
    )(
        features,
        conv_weight.reshape(3, 3 * CH, CH),
        first_weight,
        second_weight,
        out_weight.T,
        roi_count,
        roi_row,
        roi_col,
        roi_angle,
        roi_label,
        roi_target.T,
        jnp.asarray(table, bf16),
        jnp.asarray(table_t, bf16),
    )
    neck, feat_grad, second_grad, out_grad = pl.pallas_call(
        finish,
        out_shape=(
            jax.ShapeDtypeStruct((CELLS, CH), bf16),
            jax.ShapeDtypeStruct((CELLS, CH), f32),
            jax.ShapeDtypeStruct((HID, HID), f32),
            jax.ShapeDtypeStruct((OUTS, HID), f32),
        ),
        in_specs=[hbm] * 3,
        out_specs=(hbm,) * 4,
        scratch_shapes=[
            pltpu.VMEM((HID, WIDE), bf16),
            pltpu.VMEM((HID, HID), f32),
            pltpu.VMEM((OUTS, HID), f32),
            pltpu.VMEM((CELLS, CH), bf16),
            pltpu.VMEM((CELLS, CH), f32),
            dma((3, PIECES)),
            dma((3, PIECES + 1)),
        ],
        compiler_params=pltpu.CompilerParams(vmem_limit_bytes=60 * 2**20),
    )(neck, feat_grad, total)
    return (
        neck.reshape(32, 32, CH),
        feat_grad.reshape(32, 32, CH),
        second_grad,
        out_grad.T,
    )


def solution(mesh):
    in_specs = (
        P("row", "col", None),
        P(),
        P(("row", "col"), None),
        P(),
        P(),
        P(("row", "col")),
        P(("row", "col")),
        P(("row", "col")),
        P(("row", "col")),
        P(("row", "col")),
        P(("row", "col"), None),
    )
    out_specs = (P("row", "col", None), P("row", "col", None), P(), P())
    return jax.shard_map(
        on_device, mesh=mesh, in_specs=in_specs, out_specs=out_specs, check_vma=False
    )
```

```python
import heapq
import math

import jax
import jax.numpy as jnp
import numpy as np
from jax import lax
from jax.experimental import pallas as pl
from jax.experimental.pallas import tpu as pltpu
from jax.sharding import PartitionSpec as P

POOL = 7
ANGLES = 8
CLASSES = 37
OUTS = 42
HID = 1024
CH = 256
CELLS = 1024
ROIS = 256
SAMPLES = POOL * POOL
GROUP = 784
SPAN = POOL * CH
WIDE = HID + 128
COLS = WIDE // 3
MESH = pl.DeviceIdType.MESH
SLOTS = (3, 5, 7, 9, 12)

prior_logit = -4.59512

PARTS = (
    (0, 128, 256, "xyz"),
    (256, 128, 256, "yzx"),
    (512, 144, 272, "zxy"),
)


LINK = 46.5e3
DELAY = 2.2


def arrivals():
    free, events, got, order, count = {}, [], set(), [], 0
    waiting = {axis: [] for axis in "xyz"}
    opened = set()

    def push(now, axis, way, size, item):
        nonlocal count
        end = max(now, free.get((axis, way), 0.0)) + size / LINK
        free[(axis, way)] = end
        count += 1
        heapq.heappush(events, (end + DELAY, count, item))

    def send(now, item):
        part, phase, key, half, way = item
        first, cut, rows, axes = PARTS[part]
        part_rows = rows if half == 0 else cut if way == 0 else rows - cut
        push(now, axes[phase], way, part_rows * 256 * (4 if phase == 2 else 1), item)

    for item in first_sends():
        send(0.0, item)
    while events:
        now, _, item = heapq.heappop(events)
        got.add(item)
        order.append((now, item))
        for after in follow(item, got, waiting, opened):
            send(now, after)
    return order


def both(part, phase, key):
    return [(part, phase, key, 0, 0), (part, phase, key, 0, 1)]


def first_sends():
    return [item for phase in (0, 1) for part in range(3) for item in both(part, phase, 0)]


def follow(item, got, waiting, opened):
    part, phase, key, half, way = item
    sends = [(part, phase, key, 1, way)] if half == 0 else []
    lines = []
    if phase == 0:
        if half == 0:
            sends += both(part, 1, -1 if way == 0 else 1)
        elif (part, 0, 0, 1, 1 - way) in got:
            sends += both(part, 1, 2)
            lines.append(0)
    elif phase == 1:
        offsets = (0, -1, 1, 2)
        if half == 0 and all((part, 1, k, 0, way) in got for k in offsets):
            lines.append(-1 if way == 0 else 1)
        if half == 1 and all((part, 1, k, 1, w) in got for k in offsets for w in (0, 1)):
            lines.append(2)
    for line in lines:
        axis = PARTS[part][3][2]
        if axis in opened:
            sends += both(part, 2, line)
        else:
            waiting[axis].append((part, line))
    if phase == 1:
        axis = PARTS[part][3][1]
        if axis not in opened and all((part, 1, k, 0, w) in got for k in (0, -1, 1, 2) for w in (0, 1)):
            opened.add(axis)
            for other, line in waiting[axis]:
                sends += both(other, 2, line)
    return sends


def offset_tables(pool, angles):
    turn = np.arange(angles) * math.pi / angles
    along = np.arange(pool) - pool // 2
    down = (along[:, None] * np.ones((1, pool))).reshape(1, -1)
    across = (np.ones((pool, 1)) * along[None, :]).reshape(1, -1)
    cosine = np.cos(turn)[:, None]
    sine = np.sin(turn)[:, None]
    shift_rows = np.floor(down * cosine - across * sine + 0.5).astype(np.int32)
    shift_cols = np.floor(down * sine + across * cosine + 0.5).astype(np.int32)
    return (shift_rows, shift_cols)


def erf_parts(value):
    return 0.5 * (1.0 + lax.erf(value * math.sqrt(0.5)))


def slope(value, phi):
    return phi + value * jnp.exp(-0.5 * value * value) * (1.0 / math.sqrt(2.0 * math.pi))


def dot(a, b):
    return jnp.dot(a, b, preferred_element_type=jnp.float32)


def dot_nt(a, b):
    return lax.dot_general(a, b, (((1,), (1,)), ((), ())), preferred_element_type=jnp.float32)


def dot_tn(a, b):
    return lax.dot_general(a, b, (((0,), (0,)), ((), ())), preferred_element_type=jnp.float32)


def kernel(
    feat,
    conv_hbm,
    shard,
    w2_hbm,
    out_w,
    count,
    roi_row,
    roi_col,
    roi_angle,
    roi_label,
    roi_target,
    table,
    table_t,
    neck_hbm,
    grad_hbm,
    total_hbm,
    neck,
    feat_grad,
    total,
    wf,
    conv_w,
    w2,
    wo,
    facts,
    meta,
    edges,
    edge_cols,
    stage,
    slots,
    halo_row,
    halo_col,
    halo_corner,
    side,
    ext,
    taps,
    xg,
    xt,
    window,
    cells_all,
    cells_t,
    pre1,
    gp1,
    gp2,
    hid1,
    dpre2,
    dpre1,
    dxs,
    keep,
    send0,
    recv0,
    send1,
    recv1,
    keep1,
    send2,
    recv2,
    recv3,
    halo_s,
    halo_r,
    group_s,
    group_r,
    ring_s,
    ring_r,
    sib_s,
    sib_r,
    red_s,
    red_r,
    in_s,
    out_s,
):
    row = lax.axis_index("row")
    col = lax.axis_index("col")
    pos = {"x": col // 4, "y": lax.rem(col, 4), "z": row // 2}
    core = lax.rem(row, 2)

    def device(axis, step):
        at = dict(pos)
        at[axis] = lax.rem(pos[axis] + (step + 4), 4)
        return (at["z"] * 2 + core, at["x"] * 4 + at["y"])

    sibling = (row + 1 - 2 * core, col)
    member = lax.rem(col, 8)

    def group_device(step):
        return (row, col - member + lax.rem(member + step, 8))

    around = [(a, b) for a in (-1, 0, 1) for b in (-1, 0, 1) if (a, b) != (0, 0)]

    def halo_device(a, b):
        return (lax.rem(row + a + 8, 8), lax.rem(col + b + 16, 16))

    barrier = pltpu.get_barrier_semaphore()
    partners = [sibling] + [device(axis, step) for axis in "xz" for step in (1, 3)]
    partners += [group_device(step) for step in range(1, 8)]
    partners += [halo_device(a, b) for a, b in around]
    for partner in partners:
        pl.semaphore_signal(barrier, inc=1, device_id=partner, device_id_type=MESH)

    def remote(src, dst, send_sem, recv_sem, target):
        return pltpu.make_async_remote_copy(
            src_ref=src,
            dst_ref=dst,
            send_sem=send_sem,
            recv_sem=recv_sem,
            device_id=target,
            device_id_type=MESH,
        )

    loads = [
        pltpu.make_async_copy(conv_hbm, conv_w, in_s.at[0]),
        pltpu.make_async_copy(w2_hbm, w2, in_s.at[1]),
    ]
    stores = [
        pltpu.make_async_copy(neck, neck_hbm, out_s.at[0]),
        pltpu.make_async_copy(feat_grad, grad_hbm, out_s.at[1]),
    ]
    for i, first in enumerate((core * 512, 512 - core * 512)):
        rows = pl.ds(pl.multiple_of(first, 512), 512)
        stores.append(pltpu.make_async_copy(total.at[rows], total_hbm.at[rows], out_s.at[2 + i]))
    for load in loads:
        load.start()

    def group_copy(step):
        other = lax.rem(member + step, 8)
        return remote(
            stage.at[other], slots.at[member], group_s.at[step - 1], group_r.at[step - 1], group_device(step)
        )

    for m in range(8):
        stage[m, 0:98, :] = shard[:, 128 * m : 128 * m + 128]
    for i in range(32):
        cells_in_row = feat[i].astype(jnp.float32)
        edges[0, i : i + 1, :] = cells_in_row[0:1]
        edges[1, i : i + 1, :] = cells_in_row[31:32]
    edge_cols[...] = edges[...].astype(jnp.bfloat16)

    facts[...] = jnp.zeros_like(facts)
    position = lax.broadcasted_iota(jnp.int32, (1, ROIS), 1)
    angle_row = roi_angle[...].reshape(1, ROIS)
    base_row = roi_row[...].reshape(1, ROIS) * 32 + roi_col[...].reshape(1, ROIS)
    facts[0:1, :] = base_row.astype(jnp.float32)
    facts[1:2, :] = angle_row.astype(jnp.float32)
    facts[2:3, :] = roi_label[...].reshape(1, ROIS).astype(jnp.float32)
    facts[3:4, :] = jnp.where(position < count[0], 1.0, 0.0)
    facts[CLASSES:OUTS, :] = roi_target[...].astype(jnp.float32)
    meta[...] = facts[...].T
    wo[...] = jnp.zeros_like(wo)
    wo[0:OUTS, :] = out_w[...]
    lane = lax.broadcasted_iota(jnp.int32, (ROIS, 128), 1)
    angle_hot = jnp.where(lane == meta[:, 1:2].astype(jnp.int32), 1.0, 0.0).astype(jnp.bfloat16)
    cells_all[...] = dot(angle_hot, table[...]) + meta[:, 0:1]
    hot_t = jnp.where(lax.broadcasted_iota(jnp.int32, (128, ROIS), 0) == angle_row, 1.0, 0.0)
    cells_t[...] = dot(table_t[...], hot_t.astype(jnp.bfloat16)).astype(jnp.int32) + base_row

    pl.semaphore_wait(barrier, len(partners))
    group_copies = [group_copy(step) for step in range(1, 8)]
    for copy in group_copies:
        copy.start()

    def halo_copy(index):
        a, b = around[index]
        if b == 0:
            src, dst = feat.at[0 if a < 0 else 31], halo_row.at[0 if a > 0 else 1]
        elif a == 0:
            src, dst = edge_cols.at[0 if b < 0 else 1], halo_col.at[0 if b > 0 else 1]
        else:
            src = feat.at[0 if a < 0 else 31, pl.ds(0 if b < 0 else 16, 16)]
            dst = halo_corner.at[0 if a > 0 else 1, 0 if b > 0 else 1]
        return remote(src, dst, halo_s.at[index], halo_r.at[index], halo_device(a, b))

    halo_copies = [halo_copy(index) for index in range(8)]
    for copy in halo_copies:
        copy.start()

    def region(at, first, count):
        def one(axis):
            return slice(None) if at[axis] is None else at[axis]

        if at["x"] is None:
            low, high = slice(None), slice(None)
        else:
            low, high = lax.rem(at["x"], 2), at["x"] // 2
        return wf.at[low, one("y"), one("z"), core, high, pl.ds(first, count)]

    def spot(axis, step):
        return lax.rem(pos[axis] + (step + 4), 4)

    def item_copy(item):
        part, phase, key, half, way = item
        first, cut, rows, axes = PARTS[part]
        at = dict(pos)
        if phase == 1:
            at[axes[0]] = spot(axes[0], key)
        if phase == 2:
            at[axes[0]] = None
            at[axes[1]] = spot(axes[1], key)
        axis = axes[phase]
        if half == 1:
            at[axis] = spot(axis, -1 if way == 0 else 1)
            first, rows = (first, cut) if way == 0 else (first + cut, rows - cut)
        ref = region(at, first, rows)
        sem = part * 36 + (phase * 16 - 12 if phase else 0) + (key % 4) * 4 + half * 2 + way
        return remote(ref, ref, ring_s.at[sem], ring_r.at[sem], device(axis, 1 if way == 0 else -1))

    def line_copy(part, near, far):
        first, cut, rows, axes = PARTS[part]
        at = {axes[0]: None, axes[1]: spot(axes[1], near), axes[2]: spot(axes[2], far)}
        ref = region(at, first, rows)
        index = part * 4 + far % 4
        return remote(ref, ref, sib_s.at[index * 4 + near % 4], sib_r.at[index], sibling)

    def line_wait(part, far):
        first, cut, rows, axes = PARTS[part]
        at = {axes[0]: None, axes[1]: None, axes[2]: spot(axes[2], far)}
        ref = region(at, first, rows)
        pltpu.make_async_copy(ref, ref, sib_r.at[part * 4 + far % 4]).wait()

    got, waiting, opened = set(), {axis: [] for axis in "xyz"}, set()

    def arrive(item):
        item_copy(item).wait_recv()
        got.add(item)
        for after in follow(item, got, waiting, opened):
            item_copy(after).start()
        part, phase, key, half, way = item
        offsets = (0, -1, 1, 2)
        if phase == 0 and half == 1 and (part, 0, 0, 1, 1 - way) in got:
            line_copy(part, 0, 0).start()
        if phase == 1 and half == 0 and all((part, 1, k, 0, way) in got for k in offsets):
            line_copy(part, -1 if way == 0 else 1, 0).start()
        if phase == 1 and half == 1 and all((part, 1, k, 1, w) in got for k in offsets for w in (0, 1)):
            line_copy(part, 2, 0).start()
        if phase == 2 and half == 0:
            line_copy(part, key, -1 if way == 0 else 1).start()
        if phase == 2 and half == 1 and (part, 2, key, 1, 1 - way) in got:
            line_copy(part, key, 2).start()

    slots[member] = stage[member]
    for copy in group_copies:
        copy.wait_recv()
    whole = jnp.concatenate([slots[m].astype(jnp.float32)[0:98] for m in range(8)], axis=0)
    wf[lax.rem(pos["x"], 2), pos["y"], pos["z"], core, pos["x"] // 2] = whole.astype(jnp.bfloat16)
    for item in first_sends():
        item_copy(item).start()

    loads[0].wait()
    for copy in halo_copies:
        copy.wait_recv()
    zero = jnp.float32(0)
    for a in range(2):
        inside = (row > 0) if a == 0 else (row < 7)
        ext[33 * a] = jnp.where(inside, halo_row[a].astype(jnp.float32), zero).astype(jnp.bfloat16)
        for b in range(2):
            inner = inside & ((col > 0) if b == 0 else (col < 15))
            corner = halo_corner[a, b].astype(jnp.float32)
            cell = corner[15:16] if b == 0 else corner[0:1]
            place = 7 if a == 0 else 40
            side[b, place : place + 1, :] = jnp.where(inner, cell, zero)
    for b in range(2):
        inside = (col > 0) if b == 0 else (col < 15)
        side[b, 8:40, :] = jnp.where(inside, halo_col[b].astype(jnp.float32), zero)
    ext[1:33] = feat[...]
    place = lax.broadcasted_iota(jnp.int32, (32, CH), 0)

    def tap_row(i, carry):
        centre = ext[i].astype(jnp.float32)
        left = jnp.where(place == 0, side[0, pl.ds(7 + i, 1), :], pltpu.roll(centre, 1, 0))
        right = jnp.where(place == 31, side[1, pl.ds(7 + i, 1), :], pltpu.roll(centre, 31, 0))
        taps[i, :, 0:256] = left.astype(jnp.bfloat16)
        taps[i, :, 256:512] = ext[i]
        taps[i, :, 512:768] = right.astype(jnp.bfloat16)
        return carry

    lax.fori_loop(0, 34, tap_row, 0)

    def conv_rows(i, carry):
        first = i * 8
        value = jnp.zeros((256, CH), jnp.float32)
        for a in range(3):
            value = value + dot(taps[pl.ds(first + a, 8)].reshape(256, 768), conv_w[a])
        neck[pl.ds(pl.multiple_of(i * 256, 256), 256), :] = value.astype(jnp.bfloat16)
        return carry

    lax.fori_loop(0, 4, conv_rows, 0)
    stores[0].start()

    cell_lane = lax.broadcasted_iota(jnp.int32, (ROIS, CELLS), 1)

    def picked(cells, j):
        hot = jnp.where(cell_lane == cells[:, j : j + 1].astype(jnp.int32), 1.0, 0.0).astype(jnp.bfloat16)
        return dot(hot, neck[...])

    window[:, 0:256] = picked(cells_all[...], 0)
    xt[...] = jnp.zeros_like(xt)
    group_lane = lax.broadcasted_iota(jnp.int32, (ROIS, CH), 1) // 16

    def sample(g):
        cells = pltpu.roll(cells_all[...], 127 - 3 * g, 1)
        for j in range(3):
            window[:, 256 + 256 * j : 512 + 256 * j] = picked(cells, j)
        last = window[:, 768:1024]
        xt[...] = jnp.where(group_lane == g, last.astype(jnp.bfloat16), xt[...])
        far = g // 8
        shift = 16 * lax.rem(g, 8)
        back = lax.rem(128 - shift, 128)
        for i in range(6):
            low = pltpu.roll(window[:, pl.ds(pl.multiple_of(128 * (far + i), 128), 128)], back, 1)
            high = pltpu.roll(window[:, pl.ds(pl.multiple_of(128 * (far + i + 1), 128), 128)], back, 1)
            place = pl.ds(pl.multiple_of(768 * lax.rem(g, 2) + 128 * i, 128), 128)
            xg[g // 2, :, place] = jnp.where(lane < 128 - shift, low, high).astype(jnp.bfloat16)
        window[:, 0:256] = last

    def entries(z, c, high, first):
        return xg[z * 2 + c, :, pl.ds(pl.multiple_of(768 * high + first, 256), 256)]

    def product(part, far):
        axis = PARTS[part][3][2]
        here = spot(axis, far)
        line_wait(part, far)
        if axis == "z":
            pairs = [(c, high) for c in range(2) for high in range(2)]
            left = jnp.concatenate([entries(here, c, high, 0) for c, high in pairs], axis=1)
            for n in range(4):
                low, y = n // 2, 2 * (n % 2)
                halves = [
                    jnp.concatenate([wf[low, y + i, here, c, high, 0:256, :] for c, high in pairs], axis=0)
                    for i in range(2)
                ]
                pre1[:, 256 * n : 256 * n + 256] += dot(left, jnp.concatenate(halves, axis=1))
        elif axis == "x":
            low, high = lax.rem(here, 2), here // 2
            for z in range(0, 4, 2):
                pairs = [(z + i, c) for i in range(2) for c in range(2)]
                left = jnp.concatenate([entries(a, c, high, 256) for a, c in pairs], axis=1)
                for n in range(2):
                    halves = [
                        jnp.concatenate([wf[low, 2 * n + i, a, c, high, 256:512, :] for a, c in pairs], axis=0)
                        for i in range(2)
                    ]
                    cols = pl.ds(pl.multiple_of(512 * low + 256 * n, 256), 256)
                    pre1[:, cols] += dot(left, jnp.concatenate(halves, axis=1))
        else:

            def some(z, carry):
                pairs = [(c, high) for c in range(2) for high in range(2)]
                left = jnp.concatenate([entries(z, c, high, 512) for c, high in pairs], axis=1)
                halves = [
                    jnp.concatenate([wf[low, here, z, c, high, 512:768, :] for c, high in pairs], axis=0)
                    for low in range(2)
                ]
                add(dot(left, jnp.concatenate(halves, axis=1)))
                return carry

            def add(value):
                for low in range(2):
                    cols = pl.ds(pl.multiple_of(512 * low + 128 * here, 128), 128)
                    pre1[:, cols] += value[:, 128 * low : 128 * low + 128]

            lax.fori_loop(0, 4, some, 0)
            groups = [(z, c, high) for z in range(4) for c in range(2) for high in range(2)]
            halves = [
                jnp.concatenate([wf[low, here, z, c, high, 768:784, :] for z, c, high in groups], axis=0)
                for low in range(2)
            ]
            add(dot(xt[...], jnp.concatenate(halves, axis=1)))

    events = arrivals()
    now = 3.0
    batches = []
    for g in range(16):
        batches.append([])
        while events and events[0][0] <= now + 0.5:
            time, item = events.pop(0)
            now = max(now + 0.05, time)
            batches[-1].append(item)
        now += 1.1
    pre1[...] = jnp.zeros_like(pre1)

    def sample_step(g, carry):
        for index, batch in enumerate(batches):
            if batch:

                @pl.when(g == index)
                def _(batch=batch):
                    for item in batch:
                        arrive(item)

        sample(g)
        return carry

    lax.fori_loop(0, 16, sample_step, 0)
    due = {}
    for time, item in arrivals():
        part, phase, key, half, way = item
        far = 0 if phase < 2 else 2 if half else -1 if way == 0 else 1
        due[(part, far)] = max(due.get((part, far), 0.0), time + 3.0)
    todo = sorted((time, key) for key, time in due.items())
    while todo or events:
        if events and (events[0][0] <= now + 0.3 or not todo):
            time, item = events.pop(0)
            now = max(now + 0.05, time)
            arrive(item)
        elif todo and (todo[0][0] <= now or not events):
            product(*todo.pop(0)[1])
            now += 0.7
        else:
            now = min(events[0][0], todo[0][0])
    for copy in group_copies + halo_copies:
        copy.wait_send()
    for part in range(3):
        for phase in range(3):
            for key in (0, -1, 1, 2) if phase else (0,):
                for half in range(2):
                    for way in range(2):
                        item_copy((part, phase, key, half, way)).wait_send()
        for near in (0, -1, 1, 2):
            for far in (0, -1, 1, 2):
                line_copy(part, near, far).wait_send()
    loads[1].wait()

    flat = wf.reshape(8, GROUP * 16, 128)

    def weight(first, count):
        return jnp.concatenate([flat[m, pl.ds(first, count), :] for m in range(8)], axis=1)

    def activate(pre, hid, gp):
        def some(i, carry):
            rows = pl.ds(pl.multiple_of(i * 32, 32), 32)
            value = pre[rows, :]
            phi = erf_parts(value)
            if hid is not None:
                hid[rows, :] = (value * phi).astype(jnp.bfloat16)
            if gp is not None:
                gp[rows, :] = slope(value, phi)
            return carry

        lax.fori_loop(0, ROIS // 32, some, 0)

    activate(pre1, hid1, None)
    pre2 = window
    for n in range(4):
        pre2[:, 256 * n : 256 * n + 256] = dot(hid1[...], w2[:, 256 * n : 256 * n + 256])
    hid2 = dpre1
    activate(pre2, hid2, gp2)
    z = dot_nt(hid2[...], wo[...])
    label = meta[:, 2:3].astype(jnp.int32)
    live = meta[:, 3:4]
    onehot = jnp.where(lane == label, 1.0, 0.0)
    foreground = jnp.where(label < CLASSES, 1.0, 0.0)
    dlogit = 1.0 / (1.0 + jnp.exp(-(z + prior_logit))) - onehot
    dbox = jnp.clip(z - meta[...], -1.0, 1.0) * foreground
    dz = jnp.where(lane < CLASSES, dlogit, jnp.where(lane < OUTS, dbox, 0.0))
    dz = jnp.where(live > 0.5, dz, 0.0).astype(jnp.bfloat16)
    for n in range(4):
        cols = slice(256 * n, 256 * n + 256)
        dpre2[:, cols] = (dot(dz, wo[:, cols]) * gp2[:, cols]).astype(jnp.bfloat16)

    mine = pl.multiple_of(core * 512, 512)
    theirs = pl.multiple_of(512 - core * 512, 512)

    def half_grad(start, cols):
        if cols.stop <= HID:
            return dot_tn(hid1[:, pl.ds(start, 512)], dpre2[:, cols])
        return jnp.concatenate(
            [
                dot_tn(hid1[:, pl.ds(start, 512)], dpre2[:, cols.start : HID]),
                dot_tn(hid2[:, pl.ds(start, 512)], dz),
            ],
            axis=1,
        )

    def copy0(part):
        return [remote(send0.at[part], recv0.at[part], red_s.at[part], red_r.at[part], sibling)]

    for part in range(3):
        send0[part] = half_grad(theirs, slice(COLS * part, COLS * part + COLS)).astype(jnp.bfloat16)
        copy0(part)[0].start()
    for part in range(3):
        keep[part] = half_grad(mine, slice(COLS * part, COLS * part + COLS))
    activate(pre1, None, gp1)

    def order(part, level):
        return PARTS[part][3][level]

    def cols_of(part):
        return pl.ds(COLS * part, COLS)

    def scatter_copies(part, level, src, dst, rows, sems):
        copies = []
        axis = order(part, level)
        for step in (2, 1, 3):
            piece = src.at[part, pl.ds(pl.multiple_of(spot(axis, step) * rows, rows), rows)]
            sem = sems + part * 3 + step - 1
            copies.append(remote(piece, dst.at[part, step - 1], red_s.at[sem], red_r.at[sem], device(axis, step)))
        return copies

    def copy1(part):
        return scatter_copies(part, 0, send1, recv1, 128, 3)

    def copy2(part):
        return scatter_copies(part, 1, send2, recv2, 32, 12)

    def copy3(part):
        copies = []
        axis = order(part, 2)
        for step in (2, 1, 3):
            sem = 21 + part * 3 + step - 1
            ref = recv3.at[part, pos[axis]]
            copies.append(remote(ref, ref, red_s.at[sem], red_r.at[sem], device(axis, step)))
        return copies

    def rows_at(part, step):
        return pl.ds(pl.multiple_of(core * 512 + spot(order(part, 0), step) * 128, 128), 128)

    def rows_own(part):
        first = core * 512 + pos[order(part, 0)] * 128 + pos[order(part, 1)] * 32
        return pl.ds(pl.multiple_of(first, 32), 32)

    def spread_copies(part, level, rows, sems):
        copies = []
        axis = order(part, level)
        for step in (2, 1, 3):
            sem = sems + part * 3 + step - 1
            ref = total.at[rows, cols_of(part)]
            copies.append(remote(ref, ref, red_s.at[sem], red_r.at[sem], device(axis, step)))
        return copies

    def copy4(part):
        return spread_copies(part, 1, rows_own(part), 30)

    def copy5(part):
        return spread_copies(part, 0, rows_at(part, 0), 39)

    def copy6(part, step):
        ref = total.at[rows_at(part, step), cols_of(part)]
        return remote(ref, ref, red_s.at[48 + part * 4 + step], red_r.at[48], sibling)

    def start(copies):
        for copy in copies:
            copy.start()

    def wait(copies):
        for copy in copies:
            copy.wait_recv()

    def reduce_step(level, part):
        if level == 0:
            wait(copy0(part))

            for step, copy in zip((2, 1, 3, 0), copy1(part) + [None]):

                def some(i, carry):
                    first = spot(order(part, 0), step) * 128 + i * 64
                    rows = pl.ds(pl.multiple_of(first, 64), 64)
                    value = keep[part, rows, :] + recv0[part, rows, :].astype(jnp.float32)
                    if step:
                        send1[part, rows, :] = value.astype(jnp.bfloat16)
                    else:
                        keep[part, rows, :] = value
                    return carry

                lax.fori_loop(0, 2, some, 0)
                if copy is not None:
                    copy.start()
        elif level == 1:
            wait(copy1(part))
            own = pl.ds(pl.multiple_of(pos[order(part, 0)] * 128, 128), 128)
            value = keep[part, own, :]
            for step in range(3):
                value = value + recv1[part, step].astype(jnp.float32)
            keep1[part] = value
            send2[part] = value.astype(jnp.bfloat16)
            start(copy2(part))
        elif level == 2:
            wait(copy2(part))
            own = pl.ds(pl.multiple_of(pos[order(part, 1)] * 32, 32), 32)
            value = keep1[part, own, :]
            for step in range(3):
                value = value + recv2[part, step].astype(jnp.float32)
            recv3[part, pos[order(part, 2)]] = value.astype(jnp.bfloat16)
            start(copy3(part))
        elif level == 3:
            wait(copy3(part))
            value = recv3[part, 0].astype(jnp.float32)
            for step in range(1, 4):
                value = value + recv3[part, step].astype(jnp.float32)
            total[rows_own(part), cols_of(part)] = value.astype(jnp.bfloat16)
            start(copy4(part))
        elif level == 4:
            wait(copy4(part))
            start(copy5(part))
            copy6(part, 0).start()
        elif level == 5:
            for step, copy in zip((2, 1, 3), copy5(part)):
                copy.wait_recv()
                copy6(part, 4 - step).start()

    for part in range(3):
        reduce_step(0, part)

    for n in range(4):
        cols = slice(256 * n, 256 * n + 256)
        dpre1[:, cols] = (dot_nt(dpre2[...], w2[cols, :]) * gp1[:, cols]).astype(jnp.bfloat16)

    feat_grad[...] = jnp.zeros_like(feat_grad)
    cell_row = lax.broadcasted_iota(jnp.int32, (256, ROIS), 0)

    def reduce_at(k, slot):
        for level, due_slot in enumerate(SLOTS, 1):
            if due_slot % 2 == slot:

                @pl.when(k == due_slot // 2)
                def _():
                    for part in range(3):
                        reduce_step(level, part)

    def backward(k, carry):
        for j in range(POOL):
            first = pl.multiple_of(k * SPAN + 256 * j, 256)
            dxs[256 * j : 256 * j + 256, :] = dot_nt(dpre1[...], weight(first, 256)).astype(jnp.bfloat16)
        reduce_at(k, 0)
        for q in range(4):
            for j in range(POOL):
                cells = cells_t[pl.ds(k * POOL + j, 1), :] - 256 * q
                hot = jnp.where(cell_row == cells, 1.0, 0.0).astype(jnp.bfloat16)
                xg[q, :, 256 * j : 256 * j + 256] = hot
            feat_grad[256 * q : 256 * q + 256, :] += dot(xg[q], dxs[...])
        reduce_at(k, 1)
        return carry

    lax.fori_loop(0, POOL, backward, 0)
    stores[1].start()
    stores[2].start()
    half_rows = total.at[pl.ds(theirs, 512)]
    pltpu.make_async_copy(half_rows, half_rows, red_r.at[48]).wait()
    stores[3].start()
    for part in range(3):
        for make in (copy0, copy1, copy2, copy3, copy4, copy5):
            for copy in make(part):
                copy.wait_send()
        for step in range(4):
            copy6(part, step).wait_send()
    for store in stores:
        store.wait()


PIECES = 4


def finish(neck_in, grad_in, total_in, neck, feat_grad, second_grad, out_grad, total, wide, turned, cells, grads, loaded, stored):
    rows = HID // PIECES
    copies = []
    for i in range(PIECES):
        part = pl.ds(i * rows, rows)
        for n, (src, held, dst) in enumerate(
            [(total_in, total, None), (grad_in, grads, feat_grad), (neck_in, cells, neck)]
        ):
            load = pltpu.make_async_copy(src.at[part], held.at[part], loaded.at[n, i])
            load.start()
            if dst is not None:
                copies.append((load, pltpu.make_async_copy(held.at[part], dst.at[part], stored.at[n, i])))
            else:
                wide_part = pltpu.make_async_copy(wide.at[part], second_grad.at[part], stored.at[0, i])
                copies.append((load, wide_part))
    last = pltpu.make_async_copy(turned, out_grad, stored.at[0, PIECES])
    for i in range(PIECES):
        part = slice(i * rows, (i + 1) * rows)
        for n in range(3):
            load, store = copies[3 * i + n]
            load.wait()
            if n == 0:
                wide[part, :] = total[part, 0:HID].astype(jnp.float32)
                turned[:, part] = total[part, HID:].astype(jnp.float32).T[0:OUTS]
            store.start()
    last.start()
    for load, store in copies:
        store.wait()
    last.wait()


def on_device(
    features,
    conv_weight,
    first_weight,
    second_weight,
    out_weight,
    roi_count,
    roi_row,
    roi_col,
    roi_angle,
    roi_label,
    roi_target,
):
    f32, bf16 = jnp.float32, jnp.bfloat16
    shift_rows, shift_cols = offset_tables(POOL, ANGLES)
    shift = (shift_rows * 32 + shift_cols).astype(np.float32)
    table = np.zeros((128, 128), np.float32)
    table[:ANGLES, :SAMPLES] = shift
    table_t = np.ascontiguousarray(table.T[:64])

    vmem = pl.BlockSpec(memory_space=pltpu.VMEM)
    hbm = pl.BlockSpec(memory_space=pl.ANY)
    smem = pl.BlockSpec(memory_space=pltpu.SMEM)
    dma = pltpu.SemaphoreType.DMA
    neck, feat_grad, total = pl.pallas_call(
        kernel,
        out_shape=(
            jax.ShapeDtypeStruct((CELLS, CH), bf16),
            jax.ShapeDtypeStruct((CELLS, CH), f32),
            jax.ShapeDtypeStruct((HID, WIDE), bf16),
        ),
        in_specs=[vmem, hbm, vmem, hbm, vmem, smem] + [vmem] * 7,
        out_specs=(hbm, hbm, hbm),
        scratch_shapes=[
            pltpu.VMEM((CELLS, CH), bf16),
            pltpu.VMEM((CELLS, CH), f32),
            pltpu.VMEM((HID, WIDE), bf16),
            pltpu.VMEM((2, 4, 4, 2, 2, GROUP, 128), bf16),
            pltpu.VMEM((3, 3 * CH, CH), bf16),
            pltpu.VMEM((HID, HID), bf16),
            pltpu.VMEM((128, HID), bf16),
            pltpu.VMEM((128, ROIS), f32),
            pltpu.VMEM((ROIS, 128), f32),
            pltpu.VMEM((2, 32, CH), f32),
            pltpu.VMEM((2, 32, CH), bf16),
            pltpu.VMEM((8, 112, 128), bf16),
            pltpu.VMEM((8, 112, 128), bf16),
            pltpu.VMEM((2, 32, CH), bf16),
            pltpu.VMEM((2, 32, CH), bf16),
            pltpu.VMEM((2, 2, 16, CH), bf16),
            pltpu.VMEM((2, 48, CH), f32),
            pltpu.VMEM((34, 32, CH), bf16),
            pltpu.VMEM((34, 32, 3 * CH), bf16),
            pltpu.VMEM((8, ROIS, SPAN), bf16),
            pltpu.VMEM((ROIS, CH), bf16),
            pltpu.VMEM((ROIS, 1024), f32),
            pltpu.VMEM((ROIS, 128), f32),
            pltpu.VMEM((64, ROIS), jnp.int32),
            pltpu.VMEM((ROIS, HID), f32),
            pltpu.VMEM((ROIS, HID), f32),
            pltpu.VMEM((ROIS, HID), f32),
            pltpu.VMEM((ROIS, HID), bf16),
            pltpu.VMEM((ROIS, HID), bf16),
            pltpu.VMEM((ROIS, HID), bf16),
            pltpu.VMEM((SPAN, CH), bf16),
            pltpu.VMEM((3, 512, COLS), f32),
            pltpu.VMEM((3, 512, COLS), bf16),
            pltpu.VMEM((3, 512, COLS), bf16),
            pltpu.VMEM((3, 512, COLS), bf16),
            pltpu.VMEM((3, 3, 128, COLS), bf16),
            pltpu.VMEM((3, 128, COLS), f32),
            pltpu.VMEM((3, 128, COLS), bf16),
            pltpu.VMEM((3, 3, 32, COLS), bf16),
            pltpu.VMEM((3, 4, 32, COLS), bf16),
            dma((8,)),
            dma((8,)),
            dma((7,)),
            dma((7,)),
            dma((108,)),
            dma((108,)),
            dma((48,)),
            dma((12,)),
            dma((60,)),
            dma((49,)),
            dma((2,)),
            dma((4,)),
        ],
        compiler_params=pltpu.CompilerParams(
            collective_id=0, has_side_effects=True, vmem_limit_bytes=60 * 2**20
        ),
    )(
        features,
        conv_weight.reshape(3, 3 * CH, CH),
        first_weight,
        second_weight,
        out_weight.T,
        roi_count,
        roi_row,
        roi_col,
        roi_angle,
        roi_label,
        roi_target.T,
        jnp.asarray(table, bf16),
        jnp.asarray(table_t, bf16),
    )
    neck, feat_grad, second_grad, out_grad = pl.pallas_call(
        finish,
        out_shape=(
            jax.ShapeDtypeStruct((CELLS, CH), bf16),
            jax.ShapeDtypeStruct((CELLS, CH), f32),
            jax.ShapeDtypeStruct((HID, HID), f32),
            jax.ShapeDtypeStruct((OUTS, HID), f32),
        ),
        in_specs=[hbm] * 3,
        out_specs=(hbm,) * 4,
        scratch_shapes=[
            pltpu.VMEM((HID, WIDE), bf16),
            pltpu.VMEM((HID, HID), f32),
            pltpu.VMEM((OUTS, HID), f32),
            pltpu.VMEM((CELLS, CH), bf16),
            pltpu.VMEM((CELLS, CH), f32),
            dma((3, PIECES)),
            dma((3, PIECES + 1)),
        ],
        compiler_params=pltpu.CompilerParams(vmem_limit_bytes=60 * 2**20),
    )(neck, feat_grad, total)
    return (
        neck.reshape(32, 32, CH),
        feat_grad.reshape(32, 32, CH),
        second_grad,
        out_grad.T,
    )


def solution(mesh):
    in_specs = (
        P("row", "col", None),
        P(),
        P(("row", "col"), None),
        P(),
        P(),
        P(("row", "col")),
        P(("row", "col")),
        P(("row", "col")),
        P(("row", "col")),
        P(("row", "col")),
        P(("row", "col"), None),
    )
    out_specs = (P("row", "col", None), P("row", "col", None), P(), P())
    return jax.shard_map(
        on_device, mesh=mesh, in_specs=in_specs, out_specs=out_specs, check_vma=False
    )
```

```python
import heapq
import math

import jax
import jax.numpy as jnp
import numpy as np
from jax import lax
from jax.experimental import pallas as pl
from jax.experimental.pallas import tpu as pltpu
from jax.sharding import PartitionSpec as P

POOL = 7
ANGLES = 8
CLASSES = 37
OUTS = 42
HID = 1024
CH = 256
CELLS = 1024
ROIS = 256
SAMPLES = POOL * POOL
GROUP = 784
SPAN = POOL * CH
WIDE = HID + 128
COLS = WIDE // 3
MESH = pl.DeviceIdType.MESH
SLOTS = (3, 5, 7, 9, 12)

prior_logit = -4.59512

PARTS = (
    (0, 128, 256, "xyz"),
    (256, 128, 256, "yzx"),
    (512, 144, 272, "zxy"),
)


LINK = 46.5e3
DELAY = 2.2


def arrivals():
    free, events, got, order, count = {}, [], set(), [], 0
    waiting = {axis: [] for axis in "xyz"}
    opened = set()

    def push(now, axis, way, size, item):
        nonlocal count
        end = max(now, free.get((axis, way), 0.0)) + size / LINK
        free[(axis, way)] = end
        count += 1
        heapq.heappush(events, (end + DELAY, count, item))

    def send(now, item):
        part, phase, key, half, way = item
        first, cut, rows, axes = PARTS[part]
        part_rows = rows if half == 0 else cut if way == 0 else rows - cut
        push(now, axes[phase], way, part_rows * 256 * (4 if phase == 2 else 1), item)

    for item in first_sends():
        send(0.0, item)
    while events:
        now, _, item = heapq.heappop(events)
        got.add(item)
        order.append((now, item))
        for after in follow(item, got, waiting, opened):
            send(now, after)
    return order


def both(part, phase, key):
    return [(part, phase, key, 0, 0), (part, phase, key, 0, 1)]


def first_sends():
    return [item for phase in (0, 1) for part in range(3) for item in both(part, phase, 0)]


def follow(item, got, waiting, opened):
    part, phase, key, half, way = item
    sends = [(part, phase, key, 1, way)] if half == 0 else []
    lines = []
    if phase == 0:
        if half == 0:
            sends += both(part, 1, -1 if way == 0 else 1)
        elif (part, 0, 0, 1, 1 - way) in got:
            sends += both(part, 1, 2)
            lines.append(0)
    elif phase == 1:
        offsets = (0, -1, 1, 2)
        if half == 0 and all((part, 1, k, 0, way) in got for k in offsets):
            lines.append(-1 if way == 0 else 1)
        if half == 1 and all((part, 1, k, 1, w) in got for k in offsets for w in (0, 1)):
            lines.append(2)
    for line in lines:
        axis = PARTS[part][3][2]
        if axis in opened:
            sends += both(part, 2, line)
        else:
            waiting[axis].append((part, line))
    if phase == 1:
        axis = PARTS[part][3][1]
        if axis not in opened and all((part, 1, k, 0, w) in got for k in (0, -1, 1, 2) for w in (0, 1)):
            opened.add(axis)
            for other, line in waiting[axis]:
                sends += both(other, 2, line)
    return sends


def offset_tables(pool, angles):
    turn = np.arange(angles) * math.pi / angles
    along = np.arange(pool) - pool // 2
    down = (along[:, None] * np.ones((1, pool))).reshape(1, -1)
    across = (np.ones((pool, 1)) * along[None, :]).reshape(1, -1)
    cosine = np.cos(turn)[:, None]
    sine = np.sin(turn)[:, None]
    shift_rows = np.floor(down * cosine - across * sine + 0.5).astype(np.int32)
    shift_cols = np.floor(down * sine + across * cosine + 0.5).astype(np.int32)
    return (shift_rows, shift_cols)


def erf_parts(value):
    return 0.5 * (1.0 + lax.erf(value * math.sqrt(0.5)))


def slope(value, phi):
    return phi + value * jnp.exp(-0.5 * value * value) * (1.0 / math.sqrt(2.0 * math.pi))


def dot(a, b):
    return jnp.dot(a, b, preferred_element_type=jnp.float32)


def dot_nt(a, b):
    return lax.dot_general(a, b, (((1,), (1,)), ((), ())), preferred_element_type=jnp.float32)


def dot_tn(a, b):
    return lax.dot_general(a, b, (((0,), (0,)), ((), ())), preferred_element_type=jnp.float32)


def kernel(
    feat,
    conv_hbm,
    shard,
    w2_hbm,
    out_w,
    count,
    roi_row,
    roi_col,
    roi_angle,
    roi_label,
    roi_target,
    table,
    table_t,
    neck_hbm,
    grad_hbm,
    total_hbm,
    neck,
    feat_grad,
    total,
    wf,
    conv_w,
    w2,
    wo,
    facts,
    meta,
    edges,
    edge_cols,
    stage,
    slots,
    halo_row,
    halo_col,
    halo_corner,
    side,
    ext,
    taps,
    xg,
    xt,
    window,
    cells_all,
    cells_t,
    pre1,
    gp1,
    gp2,
    hid1,
    dpre2,
    dpre1,
    dxs,
    keep,
    send0,
    recv0,
    send1,
    recv1,
    keep1,
    send2,
    recv2,
    recv3,
    halo_s,
    halo_r,
    group_s,
    group_r,
    ring_s,
    ring_r,
    sib_s,
    sib_r,
    red_s,
    red_r,
    in_s,
    out_s,
):
    row = lax.axis_index("row")
    col = lax.axis_index("col")
    pos = {"x": col // 4, "y": lax.rem(col, 4), "z": row // 2}
    core = lax.rem(row, 2)

    def device(axis, step):
        at = dict(pos)
        at[axis] = lax.rem(pos[axis] + (step + 4), 4)
        return (at["z"] * 2 + core, at["x"] * 4 + at["y"])

    sibling = (row + 1 - 2 * core, col)
    member = lax.rem(col, 8)

    def group_device(step):
        return (row, col - member + lax.rem(member + step, 8))

    around = [(a, b) for a in (-1, 0, 1) for b in (-1, 0, 1) if (a, b) != (0, 0)]

    def halo_device(a, b):
        return (lax.rem(row + a + 8, 8), lax.rem(col + b + 16, 16))

    barrier = pltpu.get_barrier_semaphore()
    partners = [sibling] + [device(axis, step) for axis in "xz" for step in (1, 3)]
    partners += [group_device(step) for step in range(1, 8)]
    partners += [halo_device(a, b) for a, b in around]
    for partner in partners:
        pl.semaphore_signal(barrier, inc=1, device_id=partner, device_id_type=MESH)

    def remote(src, dst, send_sem, recv_sem, target):
        return pltpu.make_async_remote_copy(
            src_ref=src,
            dst_ref=dst,
            send_sem=send_sem,
            recv_sem=recv_sem,
            device_id=target,
            device_id_type=MESH,
        )

    loads = [
        pltpu.make_async_copy(conv_hbm, conv_w, in_s.at[0]),
        pltpu.make_async_copy(w2_hbm, w2, in_s.at[1]),
    ]
    stores = [
        pltpu.make_async_copy(neck, neck_hbm, out_s.at[0]),
        pltpu.make_async_copy(feat_grad, grad_hbm, out_s.at[1]),
    ]
    for i, first in enumerate((core * 512, 512 - core * 512)):
        rows = pl.ds(pl.multiple_of(first, 512), 512)
        stores.append(pltpu.make_async_copy(total.at[rows], total_hbm.at[rows], out_s.at[2 + i]))
    for load in loads:
        load.start()

    def group_copy(step):
        other = lax.rem(member + step, 8)
        return remote(
            stage.at[other], slots.at[member], group_s.at[step - 1], group_r.at[step - 1], group_device(step)
        )

    for m in range(8):
        stage[m, 0:98, :] = shard[:, 128 * m : 128 * m + 128]
    for i in range(32):
        cells_in_row = feat[i].astype(jnp.float32)
        edges[0, i : i + 1, :] = cells_in_row[0:1]
        edges[1, i : i + 1, :] = cells_in_row[31:32]
    edge_cols[...] = edges[...].astype(jnp.bfloat16)

    facts[...] = jnp.zeros_like(facts)
    position = lax.broadcasted_iota(jnp.int32, (1, ROIS), 1)
    angle_row = roi_angle[...].reshape(1, ROIS)
    base_row = roi_row[...].reshape(1, ROIS) * 32 + roi_col[...].reshape(1, ROIS)
    facts[0:1, :] = base_row.astype(jnp.float32)
    facts[1:2, :] = angle_row.astype(jnp.float32)
    facts[2:3, :] = roi_label[...].reshape(1, ROIS).astype(jnp.float32)
    facts[3:4, :] = jnp.where(position < count[0], 1.0, 0.0)
    facts[CLASSES:OUTS, :] = roi_target[...].astype(jnp.float32)
    meta[...] = facts[...].T
    wo[...] = jnp.zeros_like(wo)
    wo[0:OUTS, :] = out_w[...]
    lane = lax.broadcasted_iota(jnp.int32, (ROIS, 128), 1)
    angle_hot = jnp.where(lane == meta[:, 1:2].astype(jnp.int32), 1.0, 0.0).astype(jnp.bfloat16)
    cells_all[...] = dot(angle_hot, table[...]) + meta[:, 0:1]
    hot_t = jnp.where(lax.broadcasted_iota(jnp.int32, (128, ROIS), 0) == angle_row, 1.0, 0.0)
    cells_t[...] = dot(table_t[...], hot_t.astype(jnp.bfloat16)).astype(jnp.int32) + base_row

    pl.semaphore_wait(barrier, len(partners))
    group_copies = [group_copy(step) for step in range(1, 8)]
    for copy in group_copies:
        copy.start()

    def halo_copy(index):
        a, b = around[index]
        if b == 0:
            src, dst = feat.at[0 if a < 0 else 31], halo_row.at[0 if a > 0 else 1]
        elif a == 0:
            src, dst = edge_cols.at[0 if b < 0 else 1], halo_col.at[0 if b > 0 else 1]
        else:
            src = feat.at[0 if a < 0 else 31, pl.ds(0 if b < 0 else 16, 16)]
            dst = halo_corner.at[0 if a > 0 else 1, 0 if b > 0 else 1]
        return remote(src, dst, halo_s.at[index], halo_r.at[index], halo_device(a, b))

    halo_copies = [halo_copy(index) for index in range(8)]
    for copy in halo_copies:
        copy.start()

    def region(at, first, count):
        def one(axis):
            return slice(None) if at[axis] is None else at[axis]

        if at["x"] is None:
            low, high = slice(None), slice(None)
        else:
            low, high = lax.rem(at["x"], 2), at["x"] // 2
        return wf.at[low, one("y"), one("z"), core, high, pl.ds(first, count)]

    def spot(axis, step):
        return lax.rem(pos[axis] + (step + 4), 4)

    def item_copy(item):
        part, phase, key, half, way = item
        first, cut, rows, axes = PARTS[part]
        at = dict(pos)
        if phase == 1:
            at[axes[0]] = spot(axes[0], key)
        if phase == 2:
            at[axes[0]] = None
            at[axes[1]] = spot(axes[1], key)
        axis = axes[phase]
        if half == 1:
            at[axis] = spot(axis, -1 if way == 0 else 1)
            first, rows = (first, cut) if way == 0 else (first + cut, rows - cut)
        ref = region(at, first, rows)
        sem = part * 36 + (phase * 16 - 12 if phase else 0) + (key % 4) * 4 + half * 2 + way
        return remote(ref, ref, ring_s.at[sem], ring_r.at[sem], device(axis, 1 if way == 0 else -1))

    def line_copy(part, near, far):
        first, cut, rows, axes = PARTS[part]
        at = {axes[0]: None, axes[1]: spot(axes[1], near), axes[2]: spot(axes[2], far)}
        ref = region(at, first, rows)
        index = part * 4 + far % 4
        return remote(ref, ref, sib_s.at[index * 4 + near % 4], sib_r.at[index], sibling)

    def line_wait(part, far):
        first, cut, rows, axes = PARTS[part]
        at = {axes[0]: None, axes[1]: None, axes[2]: spot(axes[2], far)}
        ref = region(at, first, rows)
        pltpu.make_async_copy(ref, ref, sib_r.at[part * 4 + far % 4]).wait()

    got, waiting, opened = set(), {axis: [] for axis in "xyz"}, set()

    def arrive(item):
        item_copy(item).wait_recv()
        got.add(item)
        for after in follow(item, got, waiting, opened):
            item_copy(after).start()
        part, phase, key, half, way = item
        offsets = (0, -1, 1, 2)
        if phase == 0 and half == 1 and (part, 0, 0, 1, 1 - way) in got:
            line_copy(part, 0, 0).start()
        if phase == 1 and half == 0 and all((part, 1, k, 0, way) in got for k in offsets):
            line_copy(part, -1 if way == 0 else 1, 0).start()
        if phase == 1 and half == 1 and all((part, 1, k, 1, w) in got for k in offsets for w in (0, 1)):
            line_copy(part, 2, 0).start()
        if phase == 2 and half == 0:
            line_copy(part, key, -1 if way == 0 else 1).start()
        if phase == 2 and half == 1 and (part, 2, key, 1, 1 - way) in got:
            line_copy(part, key, 2).start()

    slots[member] = stage[member]
    for copy in group_copies:
        copy.wait_recv()
    whole = jnp.concatenate([slots[m].astype(jnp.float32)[0:98] for m in range(8)], axis=0)
    wf[lax.rem(pos["x"], 2), pos["y"], pos["z"], core, pos["x"] // 2] = whole.astype(jnp.bfloat16)
    for item in first_sends():
        item_copy(item).start()

    loads[0].wait()
    for copy in halo_copies:
        copy.wait_recv()
    zero = jnp.float32(0)
    for a in range(2):
        inside = (row > 0) if a == 0 else (row < 7)
        ext[33 * a] = jnp.where(inside, halo_row[a].astype(jnp.float32), zero).astype(jnp.bfloat16)
        for b in range(2):
            inner = inside & ((col > 0) if b == 0 else (col < 15))
            corner = halo_corner[a, b].astype(jnp.float32)
            cell = corner[15:16] if b == 0 else corner[0:1]
            place = 7 if a == 0 else 40
            side[b, place : place + 1, :] = jnp.where(inner, cell, zero)
    for b in range(2):
        inside = (col > 0) if b == 0 else (col < 15)
        side[b, 8:40, :] = jnp.where(inside, halo_col[b].astype(jnp.float32), zero)
    ext[1:33] = feat[...]
    place = lax.broadcasted_iota(jnp.int32, (32, CH), 0)

    def tap_row(i, carry):
        centre = ext[i].astype(jnp.float32)
        left = jnp.where(place == 0, side[0, pl.ds(7 + i, 1), :], pltpu.roll(centre, 1, 0))
        right = jnp.where(place == 31, side[1, pl.ds(7 + i, 1), :], pltpu.roll(centre, 31, 0))
        taps[i, :, 0:256] = left.astype(jnp.bfloat16)
        taps[i, :, 256:512] = ext[i]
        taps[i, :, 512:768] = right.astype(jnp.bfloat16)
        return carry

    lax.fori_loop(0, 34, tap_row, 0)

    def conv_rows(i, carry):
        first = i * 8
        value = jnp.zeros((256, CH), jnp.float32)
        for a in range(3):
            value = value + dot(taps[pl.ds(first + a, 8)].reshape(256, 768), conv_w[a])
        neck[pl.ds(pl.multiple_of(i * 256, 256), 256), :] = value.astype(jnp.bfloat16)
        return carry

    lax.fori_loop(0, 4, conv_rows, 0)
    stores[0].start()

    cell_lane = lax.broadcasted_iota(jnp.int32, (ROIS, CELLS), 1)

    def picked(cells, j):
        hot = jnp.where(cell_lane == cells[:, j : j + 1].astype(jnp.int32), 1.0, 0.0).astype(jnp.bfloat16)
        return dot(hot, neck[...])

    window[:, 0:256] = picked(cells_all[...], 0)
    xt[...] = jnp.zeros_like(xt)
    group_lane = lax.broadcasted_iota(jnp.int32, (ROIS, CH), 1) // 16

    def sample(g):
        cells = pltpu.roll(cells_all[...], 127 - 3 * g, 1)
        for j in range(3):
            window[:, 256 + 256 * j : 512 + 256 * j] = picked(cells, j)
        last = window[:, 768:1024]
        xt[...] = jnp.where(group_lane == g, last.astype(jnp.bfloat16), xt[...])
        far = g // 8
        shift = 16 * lax.rem(g, 8)
        back = lax.rem(128 - shift, 128)
        for i in range(6):
            low = pltpu.roll(window[:, pl.ds(pl.multiple_of(128 * (far + i), 128), 128)], back, 1)
            high = pltpu.roll(window[:, pl.ds(pl.multiple_of(128 * (far + i + 1), 128), 128)], back, 1)
            place = pl.ds(pl.multiple_of(768 * lax.rem(g, 2) + 128 * i, 128), 128)
            xg[g // 2, :, place] = jnp.where(lane < 128 - shift, low, high).astype(jnp.bfloat16)
        window[:, 0:256] = last

    def entries(z, c, high, first):
        return xg[z * 2 + c, :, pl.ds(pl.multiple_of(768 * high + first, 256), 256)]

    def product(part, far, i):
        axis = PARTS[part][3][2]
        here = spot(axis, far)
        if i == 0:
            line_wait(part, far)
        if axis == "z":
            pairs = [(c, high) for c in range(2) for high in range(2)]
            left = jnp.concatenate([entries(here, c, high, 0) for c, high in pairs], axis=1)
            low, y = i // 2, 2 * (i % 2)
            halves = [
                jnp.concatenate([wf[low, y + n, here, c, high, 0:256, :] for c, high in pairs], axis=0)
                for n in range(2)
            ]
            pre1[:, 256 * i : 256 * i + 256] += dot(left, jnp.concatenate(halves, axis=1))
        elif axis == "x":
            low, high = lax.rem(here, 2), here // 2
            z, n = 2 * (i // 2), i % 2
            pairs = [(z + a, c) for a in range(2) for c in range(2)]
            left = jnp.concatenate([entries(a, c, high, 256) for a, c in pairs], axis=1)
            halves = [
                jnp.concatenate([wf[low, 2 * n + b, a, c, high, 256:512, :] for a, c in pairs], axis=0)
                for b in range(2)
            ]
            cols = pl.ds(pl.multiple_of(512 * low + 256 * n, 256), 256)
            pre1[:, cols] += dot(left, jnp.concatenate(halves, axis=1))
        else:
            pairs = [(c, high) for c in range(2) for high in range(2)]
            left = jnp.concatenate([entries(i, c, high, 512) for c, high in pairs], axis=1)
            halves = [
                jnp.concatenate([wf[low, here, i, c, high, 512:768, :] for c, high in pairs], axis=0)
                for low in range(2)
            ]
            value = dot(left, jnp.concatenate(halves, axis=1))
            if i == 3:
                groups = [(z, c, high) for z in range(4) for c in range(2) for high in range(2)]
                halves = [
                    jnp.concatenate([wf[low, here, z, c, high, 768:784, :] for z, c, high in groups], axis=0)
                    for low in range(2)
                ]
                value = value + dot(xt[...], jnp.concatenate(halves, axis=1))
            for low in range(2):
                cols = pl.ds(pl.multiple_of(512 * low + 128 * here, 128), 128)
                pre1[:, cols] += value[:, 128 * low : 128 * low + 128]

    events = arrivals()
    now = 3.0
    batches = []
    for g in range(16):
        batches.append([])
        while events and events[0][0] <= now + 0.5:
            time, item = events.pop(0)
            now = max(now + 0.05, time)
            batches[-1].append(item)
        now += 1.1
    pre1[...] = jnp.zeros_like(pre1)

    def sample_step(g, carry):
        for index, batch in enumerate(batches):
            if batch:

                @pl.when(g == index)
                def _(batch=batch):
                    for item in batch:
                        arrive(item)

        sample(g)
        return carry

    lax.fori_loop(0, 16, sample_step, 0)
    due = {}
    for time, item in arrivals():
        part, phase, key, half, way = item
        far = 0 if phase < 2 else 2 if half else -1 if way == 0 else 1
        due[(part, far)] = max(due.get((part, far), 0.0), time + 3.0)
    todo = sorted((time, key + (i,)) for key, time in due.items() for i in range(4))
    while todo or events:
        if events and (events[0][0] <= now + 0.1 or not todo):
            time, item = events.pop(0)
            now = max(now + 0.05, time)
            arrive(item)
        elif todo and (todo[0][0] <= now or not events):
            product(*todo.pop(0)[1])
            now += 0.25
        else:
            now = min(events[0][0], todo[0][0])
    for copy in group_copies + halo_copies:
        copy.wait_send()
    for part in range(3):
        for phase in range(3):
            for key in (0, -1, 1, 2) if phase else (0,):
                for half in range(2):
                    for way in range(2):
                        item_copy((part, phase, key, half, way)).wait_send()
        for near in (0, -1, 1, 2):
            for far in (0, -1, 1, 2):
                line_copy(part, near, far).wait_send()
    loads[1].wait()

    flat = wf.reshape(8, GROUP * 16, 128)

    def weight(first, count):
        return jnp.concatenate([flat[m, pl.ds(first, count), :] for m in range(8)], axis=1)

    def activate(pre, hid, gp):
        def some(i, carry):
            rows = pl.ds(pl.multiple_of(i * 32, 32), 32)
            value = pre[rows, :]
            phi = erf_parts(value)
            if hid is not None:
                hid[rows, :] = (value * phi).astype(jnp.bfloat16)
            if gp is not None:
                gp[rows, :] = slope(value, phi)
            return carry

        lax.fori_loop(0, ROIS // 32, some, 0)

    activate(pre1, hid1, None)
    pre2 = window
    for n in range(4):
        pre2[:, 256 * n : 256 * n + 256] = dot(hid1[...], w2[:, 256 * n : 256 * n + 256])
    hid2 = dpre1
    activate(pre2, hid2, gp2)
    z = dot_nt(hid2[...], wo[...])
    label = meta[:, 2:3].astype(jnp.int32)
    live = meta[:, 3:4]
    onehot = jnp.where(lane == label, 1.0, 0.0)
    foreground = jnp.where(label < CLASSES, 1.0, 0.0)
    dlogit = 1.0 / (1.0 + jnp.exp(-(z + prior_logit))) - onehot
    dbox = jnp.clip(z - meta[...], -1.0, 1.0) * foreground
    dz = jnp.where(lane < CLASSES, dlogit, jnp.where(lane < OUTS, dbox, 0.0))
    dz = jnp.where(live > 0.5, dz, 0.0).astype(jnp.bfloat16)
    for n in range(4):
        cols = slice(256 * n, 256 * n + 256)
        dpre2[:, cols] = (dot(dz, wo[:, cols]) * gp2[:, cols]).astype(jnp.bfloat16)

    mine = pl.multiple_of(core * 512, 512)
    theirs = pl.multiple_of(512 - core * 512, 512)

    def half_grad(start, cols):
        if cols.stop <= HID:
            return dot_tn(hid1[:, pl.ds(start, 512)], dpre2[:, cols])
        return jnp.concatenate(
            [
                dot_tn(hid1[:, pl.ds(start, 512)], dpre2[:, cols.start : HID]),
                dot_tn(hid2[:, pl.ds(start, 512)], dz),
            ],
            axis=1,
        )

    def copy0(part):
        return [remote(send0.at[part], recv0.at[part], red_s.at[part], red_r.at[part], sibling)]

    for part in range(3):
        send0[part] = half_grad(theirs, slice(COLS * part, COLS * part + COLS)).astype(jnp.bfloat16)
        copy0(part)[0].start()
    for part in range(3):
        keep[part] = half_grad(mine, slice(COLS * part, COLS * part + COLS))
    activate(pre1, None, gp1)

    def order(part, level):
        return PARTS[part][3][level]

    def cols_of(part):
        return pl.ds(COLS * part, COLS)

    def scatter_copies(part, level, src, dst, rows, sems):
        copies = []
        axis = order(part, level)
        for step in (2, 1, 3):
            piece = src.at[part, pl.ds(pl.multiple_of(spot(axis, step) * rows, rows), rows)]
            sem = sems + part * 3 + step - 1
            copies.append(remote(piece, dst.at[part, step - 1], red_s.at[sem], red_r.at[sem], device(axis, step)))
        return copies

    def copy1(part):
        return scatter_copies(part, 0, send1, recv1, 128, 3)

    def copy2(part):
        return scatter_copies(part, 1, send2, recv2, 32, 12)

    def copy3(part):
        copies = []
        axis = order(part, 2)
        for step in (2, 1, 3):
            sem = 21 + part * 3 + step - 1
            ref = recv3.at[part, pos[axis]]
            copies.append(remote(ref, ref, red_s.at[sem], red_r.at[sem], device(axis, step)))
        return copies

    def rows_at(part, step):
        return pl.ds(pl.multiple_of(core * 512 + spot(order(part, 0), step) * 128, 128), 128)

    def rows_own(part):
        first = core * 512 + pos[order(part, 0)] * 128 + pos[order(part, 1)] * 32
        return pl.ds(pl.multiple_of(first, 32), 32)

    def spread_copies(part, level, rows, sems):
        copies = []
        axis = order(part, level)
        for step in (2, 1, 3):
            sem = sems + part * 3 + step - 1
            ref = total.at[rows, cols_of(part)]
            copies.append(remote(ref, ref, red_s.at[sem], red_r.at[sem], device(axis, step)))
        return copies

    def copy4(part):
        return spread_copies(part, 1, rows_own(part), 30)

    def copy5(part):
        return spread_copies(part, 0, rows_at(part, 0), 39)

    def copy6(part, step):
        ref = total.at[rows_at(part, step), cols_of(part)]
        return remote(ref, ref, red_s.at[48 + part * 4 + step], red_r.at[48], sibling)

    def start(copies):
        for copy in copies:
            copy.start()

    def wait(copies):
        for copy in copies:
            copy.wait_recv()

    def reduce_step(level, part):
        if level == 0:
            wait(copy0(part))

            for step, copy in zip((2, 1, 3, 0), copy1(part) + [None]):

                def some(i, carry):
                    first = spot(order(part, 0), step) * 128 + i * 64
                    rows = pl.ds(pl.multiple_of(first, 64), 64)
                    value = keep[part, rows, :] + recv0[part, rows, :].astype(jnp.float32)
                    if step:
                        send1[part, rows, :] = value.astype(jnp.bfloat16)
                    else:
                        keep[part, rows, :] = value
                    return carry

                lax.fori_loop(0, 2, some, 0)
                if copy is not None:
                    copy.start()
        elif level == 1:
            wait(copy1(part))
            own = pl.ds(pl.multiple_of(pos[order(part, 0)] * 128, 128), 128)
            value = keep[part, own, :]
            for step in range(3):
                value = value + recv1[part, step].astype(jnp.float32)
            keep1[part] = value
            send2[part] = value.astype(jnp.bfloat16)
            start(copy2(part))
        elif level == 2:
            wait(copy2(part))
            own = pl.ds(pl.multiple_of(pos[order(part, 1)] * 32, 32), 32)
            value = keep1[part, own, :]
            for step in range(3):
                value = value + recv2[part, step].astype(jnp.float32)
            recv3[part, pos[order(part, 2)]] = value.astype(jnp.bfloat16)
            start(copy3(part))
        elif level == 3:
            wait(copy3(part))
            value = recv3[part, 0].astype(jnp.float32)
            for step in range(1, 4):
                value = value + recv3[part, step].astype(jnp.float32)
            total[rows_own(part), cols_of(part)] = value.astype(jnp.bfloat16)
            start(copy4(part))
        elif level == 4:
            wait(copy4(part))
            start(copy5(part))
            copy6(part, 0).start()
        elif level == 5:
            for step, copy in zip((2, 1, 3), copy5(part)):
                copy.wait_recv()
                copy6(part, 4 - step).start()

    for part in range(3):
        reduce_step(0, part)

    for n in range(4):
        cols = slice(256 * n, 256 * n + 256)
        dpre1[:, cols] = (dot_nt(dpre2[...], w2[cols, :]) * gp1[:, cols]).astype(jnp.bfloat16)

    feat_grad[...] = jnp.zeros_like(feat_grad)
    cell_row = lax.broadcasted_iota(jnp.int32, (256, ROIS), 0)

    def reduce_at(k, slot):
        for level, due_slot in enumerate(SLOTS, 1):
            if due_slot % 2 == slot:

                @pl.when(k == due_slot // 2)
                def _():
                    for part in range(3):
                        reduce_step(level, part)

    def backward(k, carry):
        for j in range(POOL):
            first = pl.multiple_of(k * SPAN + 256 * j, 256)
            dxs[256 * j : 256 * j + 256, :] = dot_nt(dpre1[...], weight(first, 256)).astype(jnp.bfloat16)
        reduce_at(k, 0)
        for q in range(4):
            for j in range(POOL):
                cells = cells_t[pl.ds(k * POOL + j, 1), :] - 256 * q
                hot = jnp.where(cell_row == cells, 1.0, 0.0).astype(jnp.bfloat16)
                xg[q, :, 256 * j : 256 * j + 256] = hot
            feat_grad[256 * q : 256 * q + 256, :] += dot(xg[q], dxs[...])
        reduce_at(k, 1)
        return carry

    lax.fori_loop(0, POOL, backward, 0)
    stores[1].start()
    stores[2].start()
    half_rows = total.at[pl.ds(theirs, 512)]
    pltpu.make_async_copy(half_rows, half_rows, red_r.at[48]).wait()
    stores[3].start()
    for part in range(3):
        for make in (copy0, copy1, copy2, copy3, copy4, copy5):
            for copy in make(part):
                copy.wait_send()
        for step in range(4):
            copy6(part, step).wait_send()
    for store in stores:
        store.wait()


PIECES = 4


def finish(neck_in, grad_in, total_in, neck, feat_grad, second_grad, out_grad, total, wide, turned, cells, grads, loaded, stored):
    rows = HID // PIECES
    copies = []
    for i in range(PIECES):
        part = pl.ds(i * rows, rows)
        for n, (src, held, dst) in enumerate(
            [(total_in, total, None), (grad_in, grads, feat_grad), (neck_in, cells, neck)]
        ):
            load = pltpu.make_async_copy(src.at[part], held.at[part], loaded.at[n, i])
            load.start()
            if dst is not None:
                copies.append((load, pltpu.make_async_copy(held.at[part], dst.at[part], stored.at[n, i])))
            else:
                wide_part = pltpu.make_async_copy(wide.at[part], second_grad.at[part], stored.at[0, i])
                copies.append((load, wide_part))
    last = pltpu.make_async_copy(turned, out_grad, stored.at[0, PIECES])
    for i in range(PIECES):
        part = slice(i * rows, (i + 1) * rows)
        for n in range(3):
            load, store = copies[3 * i + n]
            load.wait()
            if n == 0:
                wide[part, :] = total[part, 0:HID].astype(jnp.float32)
                turned[:, part] = total[part, HID:].astype(jnp.float32).T[0:OUTS]
            store.start()
    last.start()
    for load, store in copies:
        store.wait()
    last.wait()


def on_device(
    features,
    conv_weight,
    first_weight,
    second_weight,
    out_weight,
    roi_count,
    roi_row,
    roi_col,
    roi_angle,
    roi_label,
    roi_target,
):
    f32, bf16 = jnp.float32, jnp.bfloat16
    shift_rows, shift_cols = offset_tables(POOL, ANGLES)
    shift = (shift_rows * 32 + shift_cols).astype(np.float32)
    table = np.zeros((128, 128), np.float32)
    table[:ANGLES, :SAMPLES] = shift
    table_t = np.ascontiguousarray(table.T[:64])

    vmem = pl.BlockSpec(memory_space=pltpu.VMEM)
    hbm = pl.BlockSpec(memory_space=pl.ANY)
    smem = pl.BlockSpec(memory_space=pltpu.SMEM)
    dma = pltpu.SemaphoreType.DMA
    neck, feat_grad, total = pl.pallas_call(
        kernel,
        out_shape=(
            jax.ShapeDtypeStruct((CELLS, CH), bf16),
            jax.ShapeDtypeStruct((CELLS, CH), f32),
            jax.ShapeDtypeStruct((HID, WIDE), bf16),
        ),
        in_specs=[vmem, hbm, vmem, hbm, vmem, smem] + [vmem] * 7,
        out_specs=(hbm, hbm, hbm),
        scratch_shapes=[
            pltpu.VMEM((CELLS, CH), bf16),
            pltpu.VMEM((CELLS, CH), f32),
            pltpu.VMEM((HID, WIDE), bf16),
            pltpu.VMEM((2, 4, 4, 2, 2, GROUP, 128), bf16),
            pltpu.VMEM((3, 3 * CH, CH), bf16),
            pltpu.VMEM((HID, HID), bf16),
            pltpu.VMEM((128, HID), bf16),
            pltpu.VMEM((128, ROIS), f32),
            pltpu.VMEM((ROIS, 128), f32),
            pltpu.VMEM((2, 32, CH), f32),
            pltpu.VMEM((2, 32, CH), bf16),
            pltpu.VMEM((8, 112, 128), bf16),
            pltpu.VMEM((8, 112, 128), bf16),
            pltpu.VMEM((2, 32, CH), bf16),
            pltpu.VMEM((2, 32, CH), bf16),
            pltpu.VMEM((2, 2, 16, CH), bf16),
            pltpu.VMEM((2, 48, CH), f32),
            pltpu.VMEM((34, 32, CH), bf16),
            pltpu.VMEM((34, 32, 3 * CH), bf16),
            pltpu.VMEM((8, ROIS, SPAN), bf16),
            pltpu.VMEM((ROIS, CH), bf16),
            pltpu.VMEM((ROIS, 1024), f32),
            pltpu.VMEM((ROIS, 128), f32),
            pltpu.VMEM((64, ROIS), jnp.int32),
            pltpu.VMEM((ROIS, HID), f32),
            pltpu.VMEM((ROIS, HID), f32),
            pltpu.VMEM((ROIS, HID), f32),
            pltpu.VMEM((ROIS, HID), bf16),
            pltpu.VMEM((ROIS, HID), bf16),
            pltpu.VMEM((ROIS, HID), bf16),
            pltpu.VMEM((SPAN, CH), bf16),
            pltpu.VMEM((3, 512, COLS), f32),
            pltpu.VMEM((3, 512, COLS), bf16),
            pltpu.VMEM((3, 512, COLS), bf16),
            pltpu.VMEM((3, 512, COLS), bf16),
            pltpu.VMEM((3, 3, 128, COLS), bf16),
            pltpu.VMEM((3, 128, COLS), f32),
            pltpu.VMEM((3, 128, COLS), bf16),
            pltpu.VMEM((3, 3, 32, COLS), bf16),
            pltpu.VMEM((3, 4, 32, COLS), bf16),
            dma((8,)),
            dma((8,)),
            dma((7,)),
            dma((7,)),
            dma((108,)),
            dma((108,)),
            dma((48,)),
            dma((12,)),
            dma((60,)),
            dma((49,)),
            dma((2,)),
            dma((4,)),
        ],
        compiler_params=pltpu.CompilerParams(
            collective_id=0, has_side_effects=True, vmem_limit_bytes=60 * 2**20
        ),
    )(
        features,
        conv_weight.reshape(3, 3 * CH, CH),
        first_weight,
        second_weight,
        out_weight.T,
        roi_count,
        roi_row,
        roi_col,
        roi_angle,
        roi_label,
        roi_target.T,
        jnp.asarray(table, bf16),
        jnp.asarray(table_t, bf16),
    )
    neck, feat_grad, second_grad, out_grad = pl.pallas_call(
        finish,
        out_shape=(
            jax.ShapeDtypeStruct((CELLS, CH), bf16),
            jax.ShapeDtypeStruct((CELLS, CH), f32),
            jax.ShapeDtypeStruct((HID, HID), f32),
            jax.ShapeDtypeStruct((OUTS, HID), f32),
        ),
        in_specs=[hbm] * 3,
        out_specs=(hbm,) * 4,
        scratch_shapes=[
            pltpu.VMEM((HID, WIDE), bf16),
            pltpu.VMEM((HID, HID), f32),
            pltpu.VMEM((OUTS, HID), f32),
            pltpu.VMEM((CELLS, CH), bf16),
            pltpu.VMEM((CELLS, CH), f32),
            dma((3, PIECES)),
            dma((3, PIECES + 1)),
        ],
        compiler_params=pltpu.CompilerParams(vmem_limit_bytes=60 * 2**20),
    )(neck, feat_grad, total)
    return (
        neck.reshape(32, 32, CH),
        feat_grad.reshape(32, 32, CH),
        second_grad,
        out_grad.T,
    )


def solution(mesh):
    in_specs = (
        P("row", "col", None),
        P(),
        P(("row", "col"), None),
        P(),
        P(),
        P(("row", "col")),
        P(("row", "col")),
        P(("row", "col")),
        P(("row", "col")),
        P(("row", "col")),
        P(("row", "col"), None),
    )
    out_specs = (P("row", "col", None), P("row", "col", None), P(), P())
    return jax.shard_map(
        on_device, mesh=mesh, in_specs=in_specs, out_specs=out_specs, check_vma=False
    )
```

```python
import heapq
import math

import jax
import jax.numpy as jnp
import numpy as np
from jax import lax
from jax.experimental import pallas as pl
from jax.experimental.pallas import tpu as pltpu
from jax.sharding import PartitionSpec as P

POOL = 7
ANGLES = 8
CLASSES = 37
OUTS = 42
HID = 1024
CH = 256
CELLS = 1024
ROIS = 256
SAMPLES = POOL * POOL
GROUP = 784
SPAN = POOL * CH
WIDE = HID + 128
COLS = WIDE // 3
MESH = pl.DeviceIdType.MESH
SLOTS = (3, 5, 7, 9, 12)

prior_logit = -4.59512

PARTS = (
    (0, 128, 256, "xyz"),
    (256, 128, 256, "yzx"),
    (512, 144, 272, "zxy"),
)


LINK = 46.5e3
DELAY = 2.2


def arrivals():
    free, events, got, order, count = {}, [], set(), [], 0
    waiting = {axis: [] for axis in "xyz"}
    opened = set()

    def push(now, axis, way, size, item):
        nonlocal count
        end = max(now, free.get((axis, way), 0.0)) + size / LINK
        free[(axis, way)] = end
        count += 1
        heapq.heappush(events, (end + DELAY, count, item))

    def send(now, item):
        part, phase, key, half, way = item
        first, cut, rows, axes = PARTS[part]
        part_rows = rows if half == 0 else cut if way == 0 else rows - cut
        push(now, axes[phase], way, part_rows * 256 * (4 if phase == 2 else 1), item)

    for item in first_sends():
        send(0.0, item)
    while events:
        now, _, item = heapq.heappop(events)
        got.add(item)
        order.append((now, item))
        for after in follow(item, got, waiting, opened):
            send(now, after)
    return order


def both(part, phase, key):
    return [(part, phase, key, 0, 0), (part, phase, key, 0, 1)]


def first_sends():
    return [item for phase in (0, 1) for part in range(3) for item in both(part, phase, 0)]


def follow(item, got, waiting, opened):
    part, phase, key, half, way = item
    sends = [(part, phase, key, 1, way)] if half == 0 else []
    lines = []
    if phase == 0:
        if half == 0:
            sends += both(part, 1, -1 if way == 0 else 1)
        elif (part, 0, 0, 1, 1 - way) in got:
            sends += both(part, 1, 2)
            lines.append(0)
    elif phase == 1:
        offsets = (0, -1, 1, 2)
        if half == 0 and all((part, 1, k, 0, way) in got for k in offsets):
            lines.append(-1 if way == 0 else 1)
        if half == 1 and all((part, 1, k, 1, w) in got for k in offsets for w in (0, 1)):
            lines.append(2)
    for line in lines:
        axis = PARTS[part][3][2]
        if axis in opened:
            sends += both(part, 2, line)
        else:
            waiting[axis].append((part, line))
    if phase == 1:
        axis = PARTS[part][3][1]
        if axis not in opened and all((part, 1, k, 0, w) in got for k in (0, -1, 1, 2) for w in (0, 1)):
            opened.add(axis)
            for other, line in waiting[axis]:
                sends += both(other, 2, line)
    return sends


def offset_tables(pool, angles):
    turn = np.arange(angles) * math.pi / angles
    along = np.arange(pool) - pool // 2
    down = (along[:, None] * np.ones((1, pool))).reshape(1, -1)
    across = (np.ones((pool, 1)) * along[None, :]).reshape(1, -1)
    cosine = np.cos(turn)[:, None]
    sine = np.sin(turn)[:, None]
    shift_rows = np.floor(down * cosine - across * sine + 0.5).astype(np.int32)
    shift_cols = np.floor(down * sine + across * cosine + 0.5).astype(np.int32)
    return (shift_rows, shift_cols)


def erf_parts(value):
    return 0.5 * (1.0 + lax.erf(value * math.sqrt(0.5)))


def slope(value, phi):
    return phi + value * jnp.exp(-0.5 * value * value) * (1.0 / math.sqrt(2.0 * math.pi))


def dot(a, b):
    return jnp.dot(a, b, preferred_element_type=jnp.float32)


def dot_nt(a, b):
    return lax.dot_general(a, b, (((1,), (1,)), ((), ())), preferred_element_type=jnp.float32)


def dot_tn(a, b):
    return lax.dot_general(a, b, (((0,), (0,)), ((), ())), preferred_element_type=jnp.float32)


def kernel(
    feat,
    conv_hbm,
    shard,
    w2_hbm,
    out_w,
    count,
    roi_row,
    roi_col,
    roi_angle,
    roi_label,
    roi_target,
    table,
    table_t,
    neck_hbm,
    grad_hbm,
    total_hbm,
    neck,
    feat_grad,
    total,
    wf,
    conv_w,
    w2,
    wo,
    facts,
    meta,
    edges,
    edge_cols,
    stage,
    slots,
    halo_row,
    halo_col,
    halo_corner,
    side,
    ext,
    taps,
    xg,
    xt,
    window,
    cells_all,
    cells_t,
    pre1,
    gp1,
    gp2,
    hid1,
    dpre2,
    dpre1,
    dxs,
    keep,
    send0,
    recv0,
    send1,
    recv1,
    keep1,
    send2,
    recv2,
    recv3,
    halo_s,
    halo_r,
    group_s,
    group_r,
    ring_s,
    ring_r,
    sib_s,
    sib_r,
    red_s,
    red_r,
    in_s,
    out_s,
):
    row = lax.axis_index("row")
    col = lax.axis_index("col")
    pos = {"x": col // 4, "y": lax.rem(col, 4), "z": row // 2}
    core = lax.rem(row, 2)

    def device(axis, step):
        at = dict(pos)
        at[axis] = lax.rem(pos[axis] + (step + 4), 4)
        return (at["z"] * 2 + core, at["x"] * 4 + at["y"])

    sibling = (row + 1 - 2 * core, col)
    member = lax.rem(col, 8)

    def group_device(step):
        return (row, col - member + lax.rem(member + step, 8))

    around = [(a, b) for a in (-1, 0, 1) for b in (-1, 0, 1) if (a, b) != (0, 0)]

    def halo_device(a, b):
        return (lax.rem(row + a + 8, 8), lax.rem(col + b + 16, 16))

    barrier = pltpu.get_barrier_semaphore()
    partners = [sibling] + [device(axis, step) for axis in "xz" for step in (1, 3)]
    partners += [group_device(step) for step in range(1, 8)]
    partners += [halo_device(a, b) for a, b in around]
    for partner in partners:
        pl.semaphore_signal(barrier, inc=1, device_id=partner, device_id_type=MESH)

    def remote(src, dst, send_sem, recv_sem, target):
        return pltpu.make_async_remote_copy(
            src_ref=src,
            dst_ref=dst,
            send_sem=send_sem,
            recv_sem=recv_sem,
            device_id=target,
            device_id_type=MESH,
        )

    loads = [
        pltpu.make_async_copy(conv_hbm, conv_w, in_s.at[0]),
        pltpu.make_async_copy(w2_hbm, w2, in_s.at[1]),
    ]
    stores = [
        pltpu.make_async_copy(neck, neck_hbm, out_s.at[0]),
        pltpu.make_async_copy(feat_grad, grad_hbm, out_s.at[1]),
    ]
    for i, first in enumerate((core * 512, 512 - core * 512)):
        rows = pl.ds(pl.multiple_of(first, 512), 512)
        stores.append(pltpu.make_async_copy(total.at[rows], total_hbm.at[rows], out_s.at[2 + i]))
    for load in loads:
        load.start()

    def group_copy(step):
        other = lax.rem(member + step, 8)
        return remote(
            stage.at[other], slots.at[member], group_s.at[step - 1], group_r.at[step - 1], group_device(step)
        )

    for m in range(8):
        stage[m, 0:98, :] = shard[:, 128 * m : 128 * m + 128]
    for i in range(32):
        cells_in_row = feat[i].astype(jnp.float32)
        edges[0, i : i + 1, :] = cells_in_row[0:1]
        edges[1, i : i + 1, :] = cells_in_row[31:32]
    edge_cols[...] = edges[...].astype(jnp.bfloat16)

    facts[...] = jnp.zeros_like(facts)
    position = lax.broadcasted_iota(jnp.int32, (1, ROIS), 1)
    angle_row = roi_angle[...].reshape(1, ROIS)
    base_row = roi_row[...].reshape(1, ROIS) * 32 + roi_col[...].reshape(1, ROIS)
    facts[0:1, :] = base_row.astype(jnp.float32)
    facts[1:2, :] = angle_row.astype(jnp.float32)
    facts[2:3, :] = roi_label[...].reshape(1, ROIS).astype(jnp.float32)
    facts[3:4, :] = jnp.where(position < count[0], 1.0, 0.0)
    facts[CLASSES:OUTS, :] = roi_target[...].astype(jnp.float32)
    meta[...] = facts[...].T
    wo[...] = jnp.zeros_like(wo)
    wo[0:OUTS, :] = out_w[...]
    lane = lax.broadcasted_iota(jnp.int32, (ROIS, 128), 1)
    angle_hot = jnp.where(lane == meta[:, 1:2].astype(jnp.int32), 1.0, 0.0).astype(jnp.bfloat16)
    cells_all[...] = dot(angle_hot, table[...]) + meta[:, 0:1]
    hot_t = jnp.where(lax.broadcasted_iota(jnp.int32, (128, ROIS), 0) == angle_row, 1.0, 0.0)
    cells_t[...] = dot(table_t[...], hot_t.astype(jnp.bfloat16)).astype(jnp.int32) + base_row

    pl.semaphore_wait(barrier, len(partners))
    group_copies = [group_copy(step) for step in range(1, 8)]
    for copy in group_copies:
        copy.start()

    def halo_copy(index):
        a, b = around[index]
        if b == 0:
            src, dst = feat.at[0 if a < 0 else 31], halo_row.at[0 if a > 0 else 1]
        elif a == 0:
            src, dst = edge_cols.at[0 if b < 0 else 1], halo_col.at[0 if b > 0 else 1]
        else:
            src = feat.at[0 if a < 0 else 31, pl.ds(0 if b < 0 else 16, 16)]
            dst = halo_corner.at[0 if a > 0 else 1, 0 if b > 0 else 1]
        return remote(src, dst, halo_s.at[index], halo_r.at[index], halo_device(a, b))

    halo_copies = [halo_copy(index) for index in range(8)]
    for copy in halo_copies:
        copy.start()

    def region(at, first, count):
        def one(axis):
            return slice(None) if at[axis] is None else at[axis]

        if at["x"] is None:
            low, high = slice(None), slice(None)
        else:
            low, high = lax.rem(at["x"], 2), at["x"] // 2
        return wf.at[low, one("y"), one("z"), core, high, pl.ds(first, count)]

    def spot(axis, step):
        return lax.rem(pos[axis] + (step + 4), 4)

    def item_copy(item):
        part, phase, key, half, way = item
        first, cut, rows, axes = PARTS[part]
        at = dict(pos)
        if phase == 1:
            at[axes[0]] = spot(axes[0], key)
        if phase == 2:
            at[axes[0]] = None
            at[axes[1]] = spot(axes[1], key)
        axis = axes[phase]
        if half == 1:
            at[axis] = spot(axis, -1 if way == 0 else 1)
            first, rows = (first, cut) if way == 0 else (first + cut, rows - cut)
        ref = region(at, first, rows)
        sem = part * 36 + (phase * 16 - 12 if phase else 0) + (key % 4) * 4 + half * 2 + way
        return remote(ref, ref, ring_s.at[sem], ring_r.at[sem], device(axis, 1 if way == 0 else -1))

    def line_copy(part, near, far):
        first, cut, rows, axes = PARTS[part]
        at = {axes[0]: None, axes[1]: spot(axes[1], near), axes[2]: spot(axes[2], far)}
        ref = region(at, first, rows)
        index = part * 4 + far % 4
        return remote(ref, ref, sib_s.at[index * 4 + near % 4], sib_r.at[index], sibling)

    def line_wait(part, far):
        first, cut, rows, axes = PARTS[part]
        at = {axes[0]: None, axes[1]: None, axes[2]: spot(axes[2], far)}
        ref = region(at, first, rows)
        pltpu.make_async_copy(ref, ref, sib_r.at[part * 4 + far % 4]).wait()

    got, waiting, opened = set(), {axis: [] for axis in "xyz"}, set()

    def arrive(item):
        item_copy(item).wait_recv()
        got.add(item)
        for after in follow(item, got, waiting, opened):
            item_copy(after).start()
        part, phase, key, half, way = item
        offsets = (0, -1, 1, 2)
        if phase == 0 and half == 1 and (part, 0, 0, 1, 1 - way) in got:
            line_copy(part, 0, 0).start()
        if phase == 1 and half == 0 and all((part, 1, k, 0, way) in got for k in offsets):
            line_copy(part, -1 if way == 0 else 1, 0).start()
        if phase == 1 and half == 1 and all((part, 1, k, 1, w) in got for k in offsets for w in (0, 1)):
            line_copy(part, 2, 0).start()
        if phase == 2 and half == 0:
            line_copy(part, key, -1 if way == 0 else 1).start()
        if phase == 2 and half == 1 and (part, 2, key, 1, 1 - way) in got:
            line_copy(part, key, 2).start()

    slots[member] = stage[member]
    for copy in group_copies:
        copy.wait_recv()
    whole = jnp.concatenate([slots[m].astype(jnp.float32)[0:98] for m in range(8)], axis=0)
    wf[lax.rem(pos["x"], 2), pos["y"], pos["z"], core, pos["x"] // 2] = whole.astype(jnp.bfloat16)
    for item in first_sends():
        item_copy(item).start()

    loads[0].wait()
    for copy in halo_copies:
        copy.wait_recv()
    zero = jnp.float32(0)
    for a in range(2):
        inside = (row > 0) if a == 0 else (row < 7)
        ext[33 * a] = jnp.where(inside, halo_row[a].astype(jnp.float32), zero).astype(jnp.bfloat16)
        for b in range(2):
            inner = inside & ((col > 0) if b == 0 else (col < 15))
            corner = halo_corner[a, b].astype(jnp.float32)
            cell = corner[15:16] if b == 0 else corner[0:1]
            place = 7 if a == 0 else 40
            side[b, place : place + 1, :] = jnp.where(inner, cell, zero)
    for b in range(2):
        inside = (col > 0) if b == 0 else (col < 15)
        side[b, 8:40, :] = jnp.where(inside, halo_col[b].astype(jnp.float32), zero)
    ext[1:33] = feat[...]
    place = lax.broadcasted_iota(jnp.int32, (32, CH), 0)

    def tap_row(i, carry):
        centre = ext[i].astype(jnp.float32)
        left = jnp.where(place == 0, side[0, pl.ds(7 + i, 1), :], pltpu.roll(centre, 1, 0))
        right = jnp.where(place == 31, side[1, pl.ds(7 + i, 1), :], pltpu.roll(centre, 31, 0))
        taps[i, :, 0:256] = left.astype(jnp.bfloat16)
        taps[i, :, 256:512] = ext[i]
        taps[i, :, 512:768] = right.astype(jnp.bfloat16)
        return carry

    lax.fori_loop(0, 34, tap_row, 0)

    def conv_rows(i, carry):
        first = i * 8
        value = jnp.zeros((256, CH), jnp.float32)
        for a in range(3):
            value = value + dot(taps[pl.ds(first + a, 8)].reshape(256, 768), conv_w[a])
        neck[pl.ds(pl.multiple_of(i * 256, 256), 256), :] = value.astype(jnp.bfloat16)
        return carry

    lax.fori_loop(0, 4, conv_rows, 0)
    stores[0].start()

    cell_lane = lax.broadcasted_iota(jnp.int32, (ROIS, CELLS), 1)

    def picked(cells, j):
        hot = jnp.where(cell_lane == cells[:, j : j + 1].astype(jnp.int32), 1.0, 0.0).astype(jnp.bfloat16)
        return dot(hot, neck[...])

    window[:, 0:256] = picked(cells_all[...], 0)
    xt[...] = jnp.zeros_like(xt)
    group_lane = lax.broadcasted_iota(jnp.int32, (ROIS, CH), 1) // 16

    def sample(g):
        cells = pltpu.roll(cells_all[...], 127 - 3 * g, 1)
        for j in range(3):
            window[:, 256 + 256 * j : 512 + 256 * j] = picked(cells, j)
        last = window[:, 768:1024]
        xt[...] = jnp.where(group_lane == g, last.astype(jnp.bfloat16), xt[...])
        far = g // 8
        shift = 16 * lax.rem(g, 8)
        back = lax.rem(128 - shift, 128)
        for i in range(6):
            low = pltpu.roll(window[:, pl.ds(pl.multiple_of(128 * (far + i), 128), 128)], back, 1)
            high = pltpu.roll(window[:, pl.ds(pl.multiple_of(128 * (far + i + 1), 128), 128)], back, 1)
            place = pl.ds(pl.multiple_of(768 * lax.rem(g, 2) + 128 * i, 128), 128)
            xg[g // 2, :, place] = jnp.where(lane < 128 - shift, low, high).astype(jnp.bfloat16)
        window[:, 0:256] = last

    def entries(z, c, high, first):
        return xg[z * 2 + c, :, pl.ds(pl.multiple_of(768 * high + first, 256), 256)]

    def product(part, far, i):
        axis = PARTS[part][3][2]
        here = spot(axis, far)
        if i == 0:
            line_wait(part, far)
        if axis == "z":
            pairs = [(c, high) for c in range(2) for high in range(2)]
            left = jnp.concatenate([entries(here, c, high, 0) for c, high in pairs], axis=1)
            low, y = i // 2, 2 * (i % 2)
            halves = [
                jnp.concatenate([wf[low, y + n, here, c, high, 0:256, :] for c, high in pairs], axis=0)
                for n in range(2)
            ]
            pre1[:, 256 * i : 256 * i + 256] += dot(left, jnp.concatenate(halves, axis=1))
        elif axis == "x":
            low, high = lax.rem(here, 2), here // 2
            z, n = 2 * (i // 2), i % 2
            pairs = [(z + a, c) for a in range(2) for c in range(2)]
            left = jnp.concatenate([entries(a, c, high, 256) for a, c in pairs], axis=1)
            halves = [
                jnp.concatenate([wf[low, 2 * n + b, a, c, high, 256:512, :] for a, c in pairs], axis=0)
                for b in range(2)
            ]
            cols = pl.ds(pl.multiple_of(512 * low + 256 * n, 256), 256)
            pre1[:, cols] += dot(left, jnp.concatenate(halves, axis=1))
        else:
            pairs = [(c, high) for c in range(2) for high in range(2)]
            left = jnp.concatenate([entries(i, c, high, 512) for c, high in pairs], axis=1)
            halves = [
                jnp.concatenate([wf[low, here, i, c, high, 512:768, :] for c, high in pairs], axis=0)
                for low in range(2)
            ]
            value = dot(left, jnp.concatenate(halves, axis=1))
            if i == 3:
                groups = [(z, c, high) for z in range(4) for c in range(2) for high in range(2)]
                halves = [
                    jnp.concatenate([wf[low, here, z, c, high, 768:784, :] for z, c, high in groups], axis=0)
                    for low in range(2)
                ]
                value = value + dot(xt[...], jnp.concatenate(halves, axis=1))
            for low in range(2):
                cols = pl.ds(pl.multiple_of(512 * low + 128 * here, 128), 128)
                pre1[:, cols] += value[:, 128 * low : 128 * low + 128]

    events = arrivals()
    now = 3.0
    batches = []
    for g in range(16):
        batches.append([])
        while events and events[0][0] <= now + 1.0:
            time, item = events.pop(0)
            now = max(now + 0.05, time)
            batches[-1].append(item)
        now += 1.1
    pre1[...] = jnp.zeros_like(pre1)

    def sample_step(g, carry):
        for index, batch in enumerate(batches):
            if batch:

                @pl.when(g == index)
                def _(batch=batch):
                    for item in batch:
                        arrive(item)

        sample(g)
        return carry

    lax.fori_loop(0, 16, sample_step, 0)
    due = {}
    for time, item in arrivals():
        part, phase, key, half, way = item
        far = 0 if phase < 2 else 2 if half else -1 if way == 0 else 1
        due[(part, far)] = max(due.get((part, far), 0.0), time + 3.0)
    todo = sorted((time, key + (i,)) for key, time in due.items() for i in range(4))
    while todo or events:
        if events and (events[0][0] <= now + 0.1 or not todo):
            time, item = events.pop(0)
            now = max(now + 0.05, time)
            arrive(item)
        elif todo and (todo[0][0] <= now or not events):
            product(*todo.pop(0)[1])
            now += 0.25
        else:
            now = min(events[0][0], todo[0][0])
    for copy in group_copies + halo_copies:
        copy.wait_send()
    for part in range(3):
        for phase in range(3):
            for key in (0, -1, 1, 2) if phase else (0,):
                for half in range(2):
                    for way in range(2):
                        item_copy((part, phase, key, half, way)).wait_send()
        for near in (0, -1, 1, 2):
            for far in (0, -1, 1, 2):
                line_copy(part, near, far).wait_send()
    loads[1].wait()

    flat = wf.reshape(8, GROUP * 16, 128)

    def weight(first, count):
        return jnp.concatenate([flat[m, pl.ds(first, count), :] for m in range(8)], axis=1)

    def activate(pre, hid, gp):
        def some(i, carry):
            rows = pl.ds(pl.multiple_of(i * 32, 32), 32)
            value = pre[rows, :]
            phi = erf_parts(value)
            if hid is not None:
                hid[rows, :] = (value * phi).astype(jnp.bfloat16)
            if gp is not None:
                gp[rows, :] = slope(value, phi)
            return carry

        lax.fori_loop(0, ROIS // 32, some, 0)

    activate(pre1, hid1, None)
    pre2 = window
    for n in range(4):
        pre2[:, 256 * n : 256 * n + 256] = dot(hid1[...], w2[:, 256 * n : 256 * n + 256])
    hid2 = dpre1
    activate(pre2, hid2, gp2)
    z = dot_nt(hid2[...], wo[...])
    label = meta[:, 2:3].astype(jnp.int32)
    live = meta[:, 3:4]
    onehot = jnp.where(lane == label, 1.0, 0.0)
    foreground = jnp.where(label < CLASSES, 1.0, 0.0)
    dlogit = 1.0 / (1.0 + jnp.exp(-(z + prior_logit))) - onehot
    dbox = jnp.clip(z - meta[...], -1.0, 1.0) * foreground
    dz = jnp.where(lane < CLASSES, dlogit, jnp.where(lane < OUTS, dbox, 0.0))
    dz = jnp.where(live > 0.5, dz, 0.0).astype(jnp.bfloat16)
    for n in range(4):
        cols = slice(256 * n, 256 * n + 256)
        dpre2[:, cols] = (dot(dz, wo[:, cols]) * gp2[:, cols]).astype(jnp.bfloat16)

    mine = pl.multiple_of(core * 512, 512)
    theirs = pl.multiple_of(512 - core * 512, 512)

    def half_grad(start, cols):
        if cols.stop <= HID:
            return dot_tn(hid1[:, pl.ds(start, 512)], dpre2[:, cols])
        return jnp.concatenate(
            [
                dot_tn(hid1[:, pl.ds(start, 512)], dpre2[:, cols.start : HID]),
                dot_tn(hid2[:, pl.ds(start, 512)], dz),
            ],
            axis=1,
        )

    def copy0(part):
        return [remote(send0.at[part], recv0.at[part], red_s.at[part], red_r.at[part], sibling)]

    for part in range(3):
        send0[part] = half_grad(theirs, slice(COLS * part, COLS * part + COLS)).astype(jnp.bfloat16)
        copy0(part)[0].start()
    for part in range(3):
        keep[part] = half_grad(mine, slice(COLS * part, COLS * part + COLS))
    activate(pre1, None, gp1)

    def order(part, level):
        return PARTS[part][3][level]

    def cols_of(part):
        return pl.ds(COLS * part, COLS)

    def scatter_copies(part, level, src, dst, rows, sems):
        copies = []
        axis = order(part, level)
        for step in (2, 1, 3):
            piece = src.at[part, pl.ds(pl.multiple_of(spot(axis, step) * rows, rows), rows)]
            sem = sems + part * 3 + step - 1
            copies.append(remote(piece, dst.at[part, step - 1], red_s.at[sem], red_r.at[sem], device(axis, step)))
        return copies

    def copy1(part):
        return scatter_copies(part, 0, send1, recv1, 128, 3)

    def copy2(part):
        return scatter_copies(part, 1, send2, recv2, 32, 12)

    def copy3(part):
        copies = []
        axis = order(part, 2)
        for step in (2, 1, 3):
            sem = 21 + part * 3 + step - 1
            ref = recv3.at[part, pos[axis]]
            copies.append(remote(ref, ref, red_s.at[sem], red_r.at[sem], device(axis, step)))
        return copies

    def rows_at(part, step):
        return pl.ds(pl.multiple_of(core * 512 + spot(order(part, 0), step) * 128, 128), 128)

    def rows_own(part):
        first = core * 512 + pos[order(part, 0)] * 128 + pos[order(part, 1)] * 32
        return pl.ds(pl.multiple_of(first, 32), 32)

    def spread_copies(part, level, rows, sems):
        copies = []
        axis = order(part, level)
        for step in (2, 1, 3):
            sem = sems + part * 3 + step - 1
            ref = total.at[rows, cols_of(part)]
            copies.append(remote(ref, ref, red_s.at[sem], red_r.at[sem], device(axis, step)))
        return copies

    def copy4(part):
        return spread_copies(part, 1, rows_own(part), 30)

    def copy5(part):
        return spread_copies(part, 0, rows_at(part, 0), 39)

    def copy6(part, step):
        ref = total.at[rows_at(part, step), cols_of(part)]
        return remote(ref, ref, red_s.at[48 + part * 4 + step], red_r.at[48], sibling)

    def start(copies):
        for copy in copies:
            copy.start()

    def wait(copies):
        for copy in copies:
            copy.wait_recv()

    def reduce_step(level, part):
        if level == 0:
            wait(copy0(part))

            for step, copy in zip((2, 1, 3, 0), copy1(part) + [None]):

                def some(i, carry):
                    first = spot(order(part, 0), step) * 128 + i * 64
                    rows = pl.ds(pl.multiple_of(first, 64), 64)
                    value = keep[part, rows, :] + recv0[part, rows, :].astype(jnp.float32)
                    if step:
                        send1[part, rows, :] = value.astype(jnp.bfloat16)
                    else:
                        keep[part, rows, :] = value
                    return carry

                lax.fori_loop(0, 2, some, 0)
                if copy is not None:
                    copy.start()
        elif level == 1:
            wait(copy1(part))
            own = pl.ds(pl.multiple_of(pos[order(part, 0)] * 128, 128), 128)
            value = keep[part, own, :]
            for step in range(3):
                value = value + recv1[part, step].astype(jnp.float32)
            keep1[part] = value
            send2[part] = value.astype(jnp.bfloat16)
            start(copy2(part))
        elif level == 2:
            wait(copy2(part))
            own = pl.ds(pl.multiple_of(pos[order(part, 1)] * 32, 32), 32)
            value = keep1[part, own, :]
            for step in range(3):
                value = value + recv2[part, step].astype(jnp.float32)
            recv3[part, pos[order(part, 2)]] = value.astype(jnp.bfloat16)
            start(copy3(part))
        elif level == 3:
            wait(copy3(part))
            value = recv3[part, 0].astype(jnp.float32)
            for step in range(1, 4):
                value = value + recv3[part, step].astype(jnp.float32)
            total[rows_own(part), cols_of(part)] = value.astype(jnp.bfloat16)
            start(copy4(part))
        elif level == 4:
            wait(copy4(part))
            start(copy5(part))
            copy6(part, 0).start()
        elif level == 5:
            for step, copy in zip((2, 1, 3), copy5(part)):
                copy.wait_recv()
                copy6(part, 4 - step).start()

    for part in range(3):
        reduce_step(0, part)

    for n in range(4):
        cols = slice(256 * n, 256 * n + 256)
        dpre1[:, cols] = (dot_nt(dpre2[...], w2[cols, :]) * gp1[:, cols]).astype(jnp.bfloat16)

    feat_grad[...] = jnp.zeros_like(feat_grad)
    cell_row = lax.broadcasted_iota(jnp.int32, (256, ROIS), 0)

    def reduce_at(k, slot):
        for level, due_slot in enumerate(SLOTS, 1):
            if due_slot % 2 == slot:

                @pl.when(k == due_slot // 2)
                def _():
                    for part in range(3):
                        reduce_step(level, part)

    def backward(k, carry):
        for j in range(POOL):
            first = pl.multiple_of(k * SPAN + 256 * j, 256)
            dxs[256 * j : 256 * j + 256, :] = dot_nt(dpre1[...], weight(first, 256)).astype(jnp.bfloat16)
        reduce_at(k, 0)
        for q in range(4):
            for j in range(POOL):
                cells = cells_t[pl.ds(k * POOL + j, 1), :] - 256 * q
                hot = jnp.where(cell_row == cells, 1.0, 0.0).astype(jnp.bfloat16)
                xg[q, :, 256 * j : 256 * j + 256] = hot
            feat_grad[256 * q : 256 * q + 256, :] += dot(xg[q], dxs[...])
        reduce_at(k, 1)
        return carry

    lax.fori_loop(0, POOL, backward, 0)
    stores[1].start()
    stores[2].start()
    half_rows = total.at[pl.ds(theirs, 512)]
    pltpu.make_async_copy(half_rows, half_rows, red_r.at[48]).wait()
    stores[3].start()
    for part in range(3):
        for make in (copy0, copy1, copy2, copy3, copy4, copy5):
            for copy in make(part):
                copy.wait_send()
        for step in range(4):
            copy6(part, step).wait_send()
    for store in stores:
        store.wait()


PIECES = 4


def finish(neck_in, grad_in, total_in, neck, feat_grad, second_grad, out_grad, total, wide, turned, cells, grads, loaded, stored):
    rows = HID // PIECES
    copies = []
    for i in range(PIECES):
        part = pl.ds(i * rows, rows)
        for n, (src, held, dst) in enumerate(
            [(total_in, total, None), (grad_in, grads, feat_grad), (neck_in, cells, neck)]
        ):
            load = pltpu.make_async_copy(src.at[part], held.at[part], loaded.at[n, i])
            load.start()
            if dst is not None:
                copies.append((load, pltpu.make_async_copy(held.at[part], dst.at[part], stored.at[n, i])))
            else:
                wide_part = pltpu.make_async_copy(wide.at[part], second_grad.at[part], stored.at[0, i])
                copies.append((load, wide_part))
    last = pltpu.make_async_copy(turned, out_grad, stored.at[0, PIECES])
    for i in range(PIECES):
        part = slice(i * rows, (i + 1) * rows)
        for n in range(3):
            load, store = copies[3 * i + n]
            load.wait()
            if n == 0:
                wide[part, :] = total[part, 0:HID].astype(jnp.float32)
                turned[:, part] = total[part, HID:].astype(jnp.float32).T[0:OUTS]
            store.start()
    last.start()
    for load, store in copies:
        store.wait()
    last.wait()


def on_device(
    features,
    conv_weight,
    first_weight,
    second_weight,
    out_weight,
    roi_count,
    roi_row,
    roi_col,
    roi_angle,
    roi_label,
    roi_target,
):
    f32, bf16 = jnp.float32, jnp.bfloat16
    shift_rows, shift_cols = offset_tables(POOL, ANGLES)
    shift = (shift_rows * 32 + shift_cols).astype(np.float32)
    table = np.zeros((128, 128), np.float32)
    table[:ANGLES, :SAMPLES] = shift
    table_t = np.ascontiguousarray(table.T[:64])

    vmem = pl.BlockSpec(memory_space=pltpu.VMEM)
    hbm = pl.BlockSpec(memory_space=pl.ANY)
    smem = pl.BlockSpec(memory_space=pltpu.SMEM)
    dma = pltpu.SemaphoreType.DMA
    neck, feat_grad, total = pl.pallas_call(
        kernel,
        out_shape=(
            jax.ShapeDtypeStruct((CELLS, CH), bf16),
            jax.ShapeDtypeStruct((CELLS, CH), f32),
            jax.ShapeDtypeStruct((HID, WIDE), bf16),
        ),
        in_specs=[vmem, hbm, vmem, hbm, vmem, smem] + [vmem] * 7,
        out_specs=(hbm, hbm, hbm),
        scratch_shapes=[
            pltpu.VMEM((CELLS, CH), bf16),
            pltpu.VMEM((CELLS, CH), f32),
            pltpu.VMEM((HID, WIDE), bf16),
            pltpu.VMEM((2, 4, 4, 2, 2, GROUP, 128), bf16),
            pltpu.VMEM((3, 3 * CH, CH), bf16),
            pltpu.VMEM((HID, HID), bf16),
            pltpu.VMEM((128, HID), bf16),
            pltpu.VMEM((128, ROIS), f32),
            pltpu.VMEM((ROIS, 128), f32),
            pltpu.VMEM((2, 32, CH), f32),
            pltpu.VMEM((2, 32, CH), bf16),
            pltpu.VMEM((8, 112, 128), bf16),
            pltpu.VMEM((8, 112, 128), bf16),
            pltpu.VMEM((2, 32, CH), bf16),
            pltpu.VMEM((2, 32, CH), bf16),
            pltpu.VMEM((2, 2, 16, CH), bf16),
            pltpu.VMEM((2, 48, CH), f32),
            pltpu.VMEM((34, 32, CH), bf16),
            pltpu.VMEM((34, 32, 3 * CH), bf16),
            pltpu.VMEM((8, ROIS, SPAN), bf16),
            pltpu.VMEM((ROIS, CH), bf16),
            pltpu.VMEM((ROIS, 1024), f32),
            pltpu.VMEM((ROIS, 128), f32),
            pltpu.VMEM((64, ROIS), jnp.int32),
            pltpu.VMEM((ROIS, HID), f32),
            pltpu.VMEM((ROIS, HID), f32),
            pltpu.VMEM((ROIS, HID), f32),
            pltpu.VMEM((ROIS, HID), bf16),
            pltpu.VMEM((ROIS, HID), bf16),
            pltpu.VMEM((ROIS, HID), bf16),
            pltpu.VMEM((SPAN, CH), bf16),
            pltpu.VMEM((3, 512, COLS), f32),
            pltpu.VMEM((3, 512, COLS), bf16),
            pltpu.VMEM((3, 512, COLS), bf16),
            pltpu.VMEM((3, 512, COLS), bf16),
            pltpu.VMEM((3, 3, 128, COLS), bf16),
            pltpu.VMEM((3, 128, COLS), f32),
            pltpu.VMEM((3, 128, COLS), bf16),
            pltpu.VMEM((3, 3, 32, COLS), bf16),
            pltpu.VMEM((3, 4, 32, COLS), bf16),
            dma((8,)),
            dma((8,)),
            dma((7,)),
            dma((7,)),
            dma((108,)),
            dma((108,)),
            dma((48,)),
            dma((12,)),
            dma((60,)),
            dma((49,)),
            dma((2,)),
            dma((4,)),
        ],
        compiler_params=pltpu.CompilerParams(
            collective_id=0, has_side_effects=True, vmem_limit_bytes=60 * 2**20
        ),
    )(
        features,
        conv_weight.reshape(3, 3 * CH, CH),
        first_weight,
        second_weight,
        out_weight.T,
        roi_count,
        roi_row,
        roi_col,
        roi_angle,
        roi_label,
        roi_target.T,
        jnp.asarray(table, bf16),
        jnp.asarray(table_t, bf16),
    )
    neck, feat_grad, second_grad, out_grad = pl.pallas_call(
        finish,
        out_shape=(
            jax.ShapeDtypeStruct((CELLS, CH), bf16),
            jax.ShapeDtypeStruct((CELLS, CH), f32),
            jax.ShapeDtypeStruct((HID, HID), f32),
            jax.ShapeDtypeStruct((OUTS, HID), f32),
        ),
        in_specs=[hbm] * 3,
        out_specs=(hbm,) * 4,
        scratch_shapes=[
            pltpu.VMEM((HID, WIDE), bf16),
            pltpu.VMEM((HID, HID), f32),
            pltpu.VMEM((OUTS, HID), f32),
            pltpu.VMEM((CELLS, CH), bf16),
            pltpu.VMEM((CELLS, CH), f32),
            dma((3, PIECES)),
            dma((3, PIECES + 1)),
        ],
        compiler_params=pltpu.CompilerParams(vmem_limit_bytes=60 * 2**20),
    )(neck, feat_grad, total)
    return (
        neck.reshape(32, 32, CH),
        feat_grad.reshape(32, 32, CH),
        second_grad,
        out_grad.T,
    )


def solution(mesh):
    in_specs = (
        P("row", "col", None),
        P(),
        P(("row", "col"), None),
        P(),
        P(),
        P(("row", "col")),
        P(("row", "col")),
        P(("row", "col")),
        P(("row", "col")),
        P(("row", "col")),
        P(("row", "col"), None),
    )
    out_specs = (P("row", "col", None), P("row", "col", None), P(), P())
    return jax.shard_map(
        on_device, mesh=mesh, in_specs=in_specs, out_specs=out_specs, check_vma=False
    )
```
